256 devices in a mesh: vocab: 64 (over z, x, core), rows: 4 (over y).
Axes of the slice: x: 4, y: 4, z: 8, core: 2. Of those that a mesh axis runs over, the one named last changes fastest.
Arguments:
- hidden: bfloat16 [1024, 4096], P(('vocab', 'rows')), may hold values from -6 to 6, as said below
- head: bfloat16 [81920, 4096], P('vocab'), as said below
- row_weight: float32 [1024], P(('vocab', 'rows')), may hold values from 30 to 300
- teacher_ids: int32 [1024, 128], P(('vocab', 'rows')), may hold values from 0 to 81919, as said below
- teacher_probs: int32 [1024, 128], P(('vocab', 'rows')), may hold values from 1 to 65409, as said below
Outputs:
- row_grad: bfloat16 [1024, 4096], P(('vocab', 'rows'))
- row_loss: float32 [1024], P(('vocab', 'rows'))
- head_grad: bfloat16 [4096, 81920], P('rows', 'vocab')
The draws below stay inside these ranges and needn't reach their ends.
Inputs may be any that keep to these rules, and one draw needn't show every extreme that they name: `teacher_ids`: each row names 128 different ids. The 4 rows of one device (an aligned block) name at most 16 ids in any one vocabulary shard (ids s * 1280 to (s + 1) * 1280 - 1), and exactly 16 in one shard. `teacher_probs`: each row's 128 values sum to exactly 65536. `hidden`: entries of order one. `head`: entries of order 3 / sqrt(4096).
All inputs are finite; a program needn't handle non-finite values.
Results may differ from the reference program's by a relative error of at most 0.024.
Values may be sent and summed in bfloat16 or wider, within the bound.
A program may use at most 128 MiB of HBM per device.

```python
import math
import jax
import jax.numpy as jnp
from jax import lax

D = 4096
VOC_DEV = 1280
TOPK = 128
ROW_DEV = 4
VOCAB = 81920
ROW_GRP = 256
ROWS = 1024
N_VOCAB = 64
N_ROWS = 4


def head_rows(key, index):

    def single(entry):
        return jax.random.normal(jax.random.fold_in(key, entry), (D,), jnp.float32)
    return jax.vmap(single)(index) * (3.0 / math.sqrt(D))


def draw_head(key, part):
    rows_all = head_rows(key, jnp.arange(VOCAB, dtype=jnp.int32))
    return rows_all.astype(jnp.bfloat16)


def draw_hidden(key, part):
    own_key = jax.random.fold_in(key, 11)
    key_base = jax.random.fold_in(own_key, 0)
    values = jax.random.normal(key_base, (ROWS, D), jnp.float32)
    return jnp.clip(values, -6.0, 6.0).astype(jnp.bfloat16)


def draw_teacher_ids(key, part):
    own_key = jax.random.fold_in(key, 23)
    key_owner, key_start, key_spread, key_shuffle = jax.random.split(own_key, 4)
    hot_count = 2 * TOPK // N_VOCAB
    blocks = ROWS // ROW_DEV
    owner_picks = jax.random.randint(key_owner, (blocks, 3), 0, N_VOCAB)
    hot_owner = jnp.repeat(jnp.min(owner_picks, axis=1), ROW_DEV)[:, None]
    hot_start = jax.random.randint(key_start, (ROWS, 1), 0, VOC_DEV)
    spread_start = jax.random.randint(key_spread, (ROWS, 1), 0, VOC_DEV)
    column = jnp.arange(TOPK, dtype=jnp.int32)[None, :]
    spread_index = jnp.maximum(column - hot_count, 0)
    owners = jnp.where(column < hot_count, hot_owner, (hot_owner + 1 + spread_index % (N_VOCAB - 1)) % N_VOCAB)
    offset = jnp.where(column < hot_count, (hot_start + column) % VOC_DEV, (spread_start + spread_index // (N_VOCAB - 1)) % VOC_DEV)
    ids_table = owners * VOC_DEV + offset
    shuffle_keys = jax.random.split(key_shuffle, ROWS)
    shuffle = jax.vmap(lambda single: jax.random.permutation(single, TOPK))(shuffle_keys)
    return jnp.take_along_axis(ids_table, shuffle, axis=1).astype(jnp.int32)


def draw_teacher_probs(key, part):
    own_key = jax.random.fold_in(key, 37)
    key_weight, key_boost, key_peak = jax.random.split(own_key, 3)
    weights_int = jax.random.randint(key_weight, (ROWS, TOPK), 1, 256)
    top_boost = jax.random.randint(key_boost, (ROWS,), 0, 8192)
    weights_int = weights_int.at[:, 0].add(top_boost)
    weight_sum = jnp.sum(weights_int, axis=1, keepdims=True)
    fixed_point = weights_int * 65536 // weight_sum
    fixed_point = fixed_point.at[:, 0].add(65536 - jnp.sum(fixed_point, axis=1))
    peak_row = jax.random.randint(key_peak, (), 0, ROWS)
    column = jnp.arange(TOPK, dtype=jnp.int32)[None, :]
    peaked = jnp.where(column == 0, 65536 - TOPK + 1, 1)
    is_peak = (jnp.arange(ROWS, dtype=jnp.int32) == peak_row)[:, None]
    fixed_point = jnp.where(is_peak, peaked, fixed_point)
    return fixed_point.astype(jnp.int32)


def block_scale(stream_key, extent, shards, least, high):
    factor_of, own = 1.0, jax.random.fold_in(stream_key, 6)
    for dim, parts in shards:
        draws = jnp.exp(jax.random.uniform(jax.random.fold_in(own, dim), (parts,), jnp.float32, least / len(shards), high / len(shards)))
        factor_of = factor_of * jnp.repeat(draws, extent[dim] // parts).reshape([-1 if axis == dim else 1 for axis in range(len(extent))])
    return factor_of


def setup_inputs(seed: int = 0) -> dict:
    keys = jax.random.split(jax.random.key(seed), 6)
    hidden = draw_hidden(jax.random.fold_in(keys[5], 71), 0)
    head = draw_head(jax.random.fold_in(keys[5], 71), 0)
    row_weight = jnp.clip(jnp.exp(math.log(300.0) - 2.3025851 * jax.random.uniform(keys[2], (ROWS,), jnp.float32) ** block_scale(keys[2], (ROWS,), ((0, 256),), -0.2, 0.2)), 30.0, 300.0)
    teacher_ids = draw_teacher_ids(jax.random.fold_in(keys[5], 71), 0)
    teacher_probs = draw_teacher_probs(jax.random.fold_in(keys[5], 71), 0)
    return {"hidden": hidden, "head": head, "row_weight": row_weight, "teacher_ids": teacher_ids, "teacher_probs": teacher_probs}


def by_group(array):
    shaped = array.reshape((N_VOCAB, N_ROWS, ROW_DEV) + array.shape[1:])
    order = (1, 0, 2) + tuple(range(3, shaped.ndim))
    return jnp.transpose(shaped, order).reshape((N_ROWS, ROW_GRP) + array.shape[1:])


def from_group(array):
    shaped = array.reshape((N_ROWS, N_VOCAB, ROW_DEV) + array.shape[2:])
    order = (1, 0, 2) + tuple(range(3, shaped.ndim))
    return jnp.transpose(shaped, order).reshape((ROWS,) + array.shape[2:])


def reference(hidden, head, row_weight, teacher_ids, teacher_probs):
    def group_step(total, items):
        group_hidden, group_weight, group_ids, group_probs = items
        logits = jnp.dot(group_hidden, head.T, preferred_element_type=jnp.float32)
        largest = jnp.max(logits, axis=1)
        shifted = jnp.exp(logits - largest[:, None])
        row_total = jnp.sum(shifted, axis=1)
        row_index = jnp.broadcast_to(jnp.arange(ROW_GRP, dtype=jnp.int32)[:, None], group_ids.shape)
        teacher = jnp.zeros((ROW_GRP, VOCAB), jnp.float32).at[row_index, group_ids].add(
            group_probs.astype(jnp.float32) / 65536.0)
        grad_logits = (group_weight[:, None] * (shifted / row_total[:, None] - teacher)).astype(jnp.bfloat16)
        row_grad = jnp.dot(grad_logits, head, preferred_element_type=jnp.float32).astype(jnp.bfloat16)
        row_loss = largest + jnp.log(row_total) - jnp.sum(teacher * logits, axis=1)
        head_part = jnp.dot(group_hidden.T, grad_logits, preferred_element_type=jnp.float32).astype(jnp.bfloat16)
        return total + head_part.astype(jnp.float32), (row_grad, row_loss)

    start = jnp.zeros((D, VOCAB), jnp.float32)
    items = (by_group(hidden), by_group(row_weight), by_group(teacher_ids), by_group(teacher_probs))
    total, (grads, losses) = lax.scan(group_step, start, items)
    return from_group(grads), from_group(losses), total.astype(jnp.bfloat16)
```

```python
import jax
import jax.numpy as jnp
from jax import lax
from jax.experimental import pallas as pl
from jax.experimental.pallas import tpu as pltpu
from jax.sharding import PartitionSpec as P

MESH = pl.DeviceIdType.MESH
BF, F32, I32 = jnp.bfloat16, jnp.float32, jnp.int32
NZ, NX, NC, NY = 8, 4, 2, 4
D, VOC, TOPK = 4096, 1280, 128
GRP = 256
SLOTS = 16
DS = D // NY
Q = 4
QW = D // Q
YC = 2
YW = VOC // YC


def iota(shape, dim):
    return lax.broadcasted_iota(I32, shape, dim)


def kernel(
    hidden, head_hbm, weight, ids, probs,
    row_out, loss_out, head_out,
    head, own16, xbuf, hid, meta_own, meta, hy,
    logits, e_buf, teacher, packet, st1, st2, cols,
    g_buf, gp, part, p_send, p_recv, s1, x_send, x_recv, z_f32, z_send, z_recv,
    acc, stage,
    sem_head, sem_out,
    x_s, x_r, xm_s, xm_r, ring_s, ring_r, zm_s, zm_r, sib_s, sib_r, sm_s, sm_r,
    hy_s, hy_r, hs_s, hs_r, st1_s, st1_r, st2_s, st2_r, y_s, y_r,
    rp_s, rp_r, rx_s, rx_r, rz_s, rz_r,
):
    v, y = lax.axis_index("vocab"), lax.axis_index("rows")
    z, x, c = lax.div(v, 8), lax.rem(lax.div(v, 2), 4), lax.rem(v, 2)
    oc = 1 - c

    def dev(dz=0, dx=0, dc=0, dy=0):
        zz = lax.rem(z + dz, NZ)
        xx = lax.rem(x + dx, NX)
        cc = c if dc == 0 else oc
        return (zz * 8 + xx * 2 + cc, lax.rem(y + dy, NY))

    started = []

    def send(src, dst, ss, rs, to):
        copy = pltpu.make_async_remote_copy(
            src_ref=src, dst_ref=dst, send_sem=ss, recv_sem=rs, device_id=to, device_id_type=MESH
        )
        copy.start()
        started.append(copy)
        return copy

    head_in = []
    for i in range(5):
        part_rows = pl.ds(i * 256, 256)
        copy = pltpu.make_async_copy(head_hbm.at[part_rows], head.at[part_rows], sem_head.at[i])
        copy.start()
        head_in.append(copy)

    xc = [(dx, dc) for dx in range(NX) for dc in range(NC) if (dx, dc) != (0, 0)]
    barrier = pltpu.get_barrier_semaphore()
    peers = [dev(dx=dx, dc=dc) for dx, dc in xc]
    peers += [dev(dz=d) for d in range(1, NZ)]
    peers += [dev(dy=d) for d in range(1, NY)]
    for to in peers:
        pl.semaphore_signal(barrier, inc=1, device_id=to, device_id_type=MESH)

    h = hidden[...].astype(F32)
    own16[...] = jnp.concatenate([h[:, q * QW:(q + 1) * QW] for q in range(Q)], axis=0).astype(BF)
    meta_own[0:4, :] = ids[...]
    meta_own[4:8, :] = probs[...]
    pl.semaphore_wait(barrier, len(peers))

    got = [send(own16, xbuf.at[x], x_s.at[d - 1], x_r.at[d - 1], dev(dx=d)) for d in (1, 3, 2)]
    base = c * 8 + z
    blk = base * 4 + x
    got_m = [send(meta_own, meta.at[blk], xm_s.at[d - 1], xm_r.at[d - 1], dev(dx=d)) for d in (1, 3, 2)]
    xbuf[x] = own16[...]
    meta[blk] = meta_own[...]
    for copy in got:
        copy.wait_recv()
    row0 = pl.multiple_of(base * 16, 16)
    blocks = [xbuf[i].astype(F32) for i in range(NX)]
    for q in range(Q):
        hid[pl.ds(row0, 16), q * QW:(q + 1) * QW] = jnp.concatenate(
            [b[4 * q:4 * q + 4] for b in blocks], axis=0
        ).astype(BF)

    def tile(zz):
        return hid.at[pl.ds(pl.multiple_of((c * 8 + zz) * 16, 16), 16)]

    def ring_send(way, step):
        zz = lax.rem(z + (NZ - step if way == 0 else step), NZ)
        ref = tile(zz)
        return send(ref, ref, ring_s.at[way, step], ring_r.at[way, step], dev(dz=1 if way == 0 else NZ - 1))

    sib = []

    def sib_send(zz):
        ref, n = tile(zz), len(sib)
        sib.append(send(ref, ref, sib_s.at[n], sib_r.at[n], dev(dc=1)))

    now = [ring_send(0, 0), ring_send(1, 0)]
    sib_send(z)
    for copy in got_m:
        copy.wait_recv()

    def meta_tile(zz):
        return meta.at[pl.ds((c * 8 + zz) * 4, 4)]

    own_meta = meta_tile(z)
    got_m = [send(own_meta, own_meta, zm_s.at[d - 1], zm_r.at[d - 1], dev(dz=d)) for d in range(1, NZ)]
    for step in range(1, 5):
        for way in range(2):
            if way == 1 and step == 4:
                continue
            now[way].wait_recv()
            if step < (4 if way == 0 else 3):
                now[way] = ring_send(way, step)
            sib_send(lax.rem(z + (NZ - step if way == 0 else step), NZ))

    half = pl.ds(pl.multiple_of(c * 128, 128), 128)
    got_hy = {}
    for d in (1, 3, 2):
        yy = lax.rem(y + d, NY)
        src = hid.at[half, pl.ds(pl.multiple_of(yy * DS, DS), DS)]
        got_hy[d] = send(src, hy.at[d - 1, half], hy_s.at[d - 1], hy_r.at[d - 1], dev(dy=d))

    for copy in got_m:
        copy.wait_recv()
    half_meta = meta.at[pl.ds(c * 32, 32)]
    got_sm = send(half_meta, half_meta, sm_s, sm_r, dev(dc=1))
    got_sm.wait_recv()

    first = v * VOC
    all_meta = meta[...]
    off = all_meta[:, 0:4, :].reshape(GRP, TOPK) - first
    prob = all_meta[:, 4:8, :].reshape(GRP, TOPK)
    mine = jnp.logical_and(off >= 0, off < VOC)
    mask = jnp.where(mine, 1.0, 0.0).astype(BF)
    before = jnp.where(iota((TOPK, TOPK), 0) < iota((TOPK, TOPK), 1), 1.0, 0.0).astype(BF)
    ri, rj = iota((GRP, GRP), 0), iota((GRP, GRP), 1)
    earlier = jnp.where(jnp.logical_and((ri >> 2) == (rj >> 2), rj < ri), 1.0, 0.0).astype(BF)
    count = jnp.dot(mask, jnp.ones((TOPK, TOPK), BF), preferred_element_type=F32).astype(BF)
    rank = jnp.dot(mask, before, preferred_element_type=F32)
    rank = rank + jnp.dot(earlier, count, preferred_element_type=F32)
    rank = jnp.where(mine, rank, -1.0).reshape(64, 4, TOPK)
    rows4 = iota((GRP, TOPK), 0) & 3
    code = (off * 4 + rows4).astype(F32).reshape(64, 4, TOPK)
    probf = prob.astype(F32).reshape(64, 4, TOPK)
    slot = iota((64, SLOTS, TOPK), 1).astype(F32)
    code_at = jnp.zeros((64, SLOTS, TOPK), F32)
    prob_at = jnp.zeros((64, SLOTS, TOPK), F32)
    for r in range(4):
        hit = rank[:, r:r + 1, :] == slot
        code_at = code_at + jnp.where(hit, code[:, r:r + 1, :], 0.0)
        prob_at = prob_at + jnp.where(hit, probf[:, r:r + 1, :], 0.0)
    code_i = jnp.sum(code_at, axis=2, keepdims=True).reshape(64 * SLOTS, 1).astype(I32)
    prob_i = jnp.sum(prob_at, axis=2, keepdims=True).reshape(64 * SLOTS, 1).astype(I32)
    lanes = iota((256, 128), 1)
    places = iota((256, VOC), 1)
    block_row = (iota((256, 128), 0) >> 4) << 2
    for b in range(4):
        code_b, prob_b = code_i[b * 256:(b + 1) * 256], prob_i[b * 256:(b + 1) * 256]
        one_hot = jnp.where((code_b >> 2) == places, 1.0, 0.0).astype(BF)
        byte = jnp.where(lanes < 64, prob_b >> 8, prob_b & 255).astype(F32)
        at = jnp.where((lanes & 63) == block_row + (code_b & 3), byte, 0.0).astype(BF)
        both = lax.dot_general(at, one_hot, (((0,), (0,)), ((), ())), preferred_element_type=F32)
        teacher[b * 64:(b + 1) * 64, :] = (both[0:64] * 256.0 + both[64:128]) * (1.0 / 65536.0)

    for copy in head_in:
        copy.wait()
    for copy in sib:
        copy.wait_recv()

    for n in range(5):
        ns = slice(n * 256, (n + 1) * 256)
        logits[:, ns] = lax.dot_general(
            hid[...], head[ns, :], (((1,), (1,)), ((), ())), preferred_element_type=F32
        )
    lg = logits[...]
    m_own = jnp.max(lg, axis=1, keepdims=True)
    ex = jnp.exp(lg - m_own)
    e_buf[...] = ex
    s_own = jnp.sum(ex, axis=1, keepdims=True)
    t_own = jnp.sum(teacher[...] * lg, axis=1, keepdims=True)
    my_row = blk * 4
    row_id = iota((GRP, 128), 0)
    lane = iota((GRP, 128), 1)
    w_own = jnp.zeros((GRP, 128), F32)
    for r in range(4):
        w_own = jnp.where(row_id == my_row + r, weight[r], w_own)
    wide = jnp.where(lane == 0, m_own, jnp.where(lane == 1, s_own, jnp.where(lane == 2, w_own, t_own)))
    packet[...] = wide.T[0:8, :]

    def combine(buf):
        top = buf[0, 0:1, :]
        for i in range(1, 8):
            top = jnp.maximum(top, buf[i, 0:1, :])
        total = [jnp.zeros((1, GRP), F32) for _ in range(3)]
        for i in range(8):
            total[0] = total[0] + buf[i, 1:2, :] * jnp.exp(buf[i, 0:1, :] - top)
            total[1] = total[1] + buf[i, 2:3, :]
            total[2] = total[2] + buf[i, 3:4, :]
        sub = iota((8, GRP), 0)
        return jnp.where(
            sub == 0, top, jnp.where(sub == 1, total[0], jnp.where(sub == 2, total[1], total[2]))
        )

    place = x * 2 + c
    got = [
        send(packet, st1.at[place], st1_s.at[i], st1_r.at[i], dev(dx=dx, dc=dc))
        for i, (dx, dc) in enumerate(xc)
    ]
    st1[place] = packet[...]
    for copy in got:
        copy.wait_recv()
    st2[z] = combine(st1)
    mid = st2.at[z]
    got = [send(mid, mid, st2_s.at[d - 1], st2_r.at[d - 1], dev(dz=d)) for d in range(1, NZ)]
    for copy in got:
        copy.wait_recv()
    final = combine(st2)
    cols[...] = jnp.concatenate([final, jnp.zeros((120, GRP), F32)], axis=0).T
    top_c, total_c, w_c = cols[:, 0:1], cols[:, 1:2], cols[:, 2:3]
    scale = jnp.exp(m_own - top_c) / total_c
    g_buf[0] = (w_c * (e_buf[...] * scale - teacher[...])).astype(BF)

    own_cols = cols[pl.ds(pl.multiple_of(my_row, 4), 4), :]
    loss_out[...] = own_cols[:, 0:1] + jnp.log(own_cols[:, 1:2]) - own_cols[:, 3:4] + jnp.zeros((4, 128), F32)

    got_y = {}
    for k in range(YC):
        ks = pl.ds(k * YW, YW)
        for d in (1, 3, 2):
            got_y[d, k] = send(
                g_buf.at[0, :, ks], g_buf.at[d, :, ks], y_s.at[d - 1, k], y_r.at[d - 1, k], dev(dy=d)
            )

    i0 = iota((GRP, GRP), 0)
    src = ((i0 >> 7) << 7) + (((i0 >> 2) & 7) << 4) + (((i0 >> 5) & 3) << 2) + (i0 & 3)
    perm = jnp.where(src == iota((GRP, GRP), 1), 1.0, 0.0).astype(BF)
    gp[...] = jnp.dot(perm, g_buf[0], preferred_element_type=F32).astype(BF)
    other = pl.ds(pl.multiple_of(oc * 128, 128), 128)
    got_p, got_x, got_z = {}, {}, {}

    def pair_stage(q):
        part[q % 2] = jnp.dot(gp[...], head[:, q * QW:(q + 1) * QW], preferred_element_type=F32)
        p_send[q] = part[q % 2, other, :].astype(BF)
        got_p[q] = send(p_send.at[q], p_recv.at[q], rp_s.at[q], rp_r.at[q], dev(dc=1))

    def x_stage(q):
        got_p[q].wait_recv()
        s1[q] = part[q % 2, half, :] + p_recv[q].astype(F32)
        x_send[q] = s1[q].astype(BF)
        for d in (1, 3, 2):
            xx = lax.rem(x + d, NX)
            rows = pl.ds(pl.multiple_of(xx * 32, 32), 32)
            got_x[q, d] = send(
                x_send.at[q, rows], x_recv.at[q, d - 1], rx_s.at[q, d - 1], rx_r.at[q, d - 1], dev(dx=d)
            )

    def z_stage(q):
        for d in (1, 3, 2):
            got_x[q, d].wait_recv()
        s2 = s1[q, pl.ds(pl.multiple_of(x * 32, 32), 32), :]
        for d in range(3):
            s2 = s2 + x_recv[q, d].astype(F32)
        for zz in range(NZ):
            piece = jnp.concatenate([s2[4 * zz:4 * zz + 4, i * 256:(i + 1) * 256] for i in range(4)], axis=0)
            z_f32[q, zz] = piece
            z_send[q, zz] = piece.astype(BF)
        for d in range(1, NZ):
            zz = lax.rem(z + d, NZ)
            got_z[q, d] = send(
                z_send.at[q, zz], z_recv.at[q, d - 1], rz_s.at[q, d - 1], rz_r.at[q, d - 1], dev(dz=d)
            )

    def last_stage(q):
        for d in range(1, NZ):
            got_z[q, d].wait_recv()
        total = z_f32[q, z]
        for d in range(NZ - 1):
            total = total + z_recv[q, d].astype(F32)
        row_out[:, q * QW:(q + 1) * QW] = jnp.concatenate(
            [total[4 * i:4 * i + 4] for i in range(4)], axis=1
        ).astype(BF)

    def head_step(d, k):
        ks = slice(k * YW, (k + 1) * YW)
        if d == 0:
            left = hid[:, pl.ds(pl.multiple_of(y * DS, DS), DS)]
        else:
            left = hy[d - 1]
            got_y[d, k].wait_recv()
        term = lax.dot_general(
            left, g_buf[d, :, ks], (((0,), (0,)), ((), ())), preferred_element_type=F32
        )
        if d == 0:
            acc[:, ks] = term
        elif d != 2:
            acc[:, ks] += term
        else:
            stage[:, ks] = (acc[:, ks] + term).astype(BF)

    pair_stage(0)
    pair_stage(1)
    x_stage(0)
    pair_stage(2)
    x_stage(1)
    pair_stage(3)
    x_stage(2)
    x_stage(3)
    got_hs = []
    for d in (1, 3, 2):
        got_hy[d].wait_recv()
        ref = hy.at[d - 1, half]
        got_hs.append(send(ref, ref, hs_s.at[d - 1], hs_r.at[d - 1], dev(dc=1)))
    z_stage(0)
    z_stage(1)
    head_step(0, 0)
    head_step(0, 1)
    z_stage(2)
    z_stage(3)
    for copy in got_hs:
        copy.wait_recv()
    for d in (1, 3):
        for k in range(YC):
            head_step(d, k)
    for q in range(Q):
        last_stage(q)
    outs = []
    for k in range(YC):
        head_step(2, k)
        ks = pl.ds(k * YW, YW)
        copy = pltpu.make_async_copy(stage.at[:, ks], head_out.at[:, ks], sem_out.at[k])
        copy.start()
        outs.append(copy)
    for copy in started:
        copy.wait_send()
    for copy in outs:
        copy.wait()


def shards(hidden, head, row_weight, teacher_ids, teacher_probs):
    dma = pltpu.SemaphoreType.DMA
    vm = pltpu.VMEM
    any_spec = pl.BlockSpec(memory_space=pl.ANY)
    vm_spec = pl.BlockSpec(memory_space=pltpu.VMEM)
    row_grad, loss, head_grad = pl.pallas_call(
        kernel,
        out_shape=(
            jax.ShapeDtypeStruct((4, D), BF),
            jax.ShapeDtypeStruct((4, 128), F32),
            jax.ShapeDtypeStruct((DS, VOC), BF),
        ),
        in_specs=[vm_spec, any_spec, pl.BlockSpec(memory_space=pltpu.SMEM), vm_spec, vm_spec],
        out_specs=(vm_spec, vm_spec, any_spec),
        scratch_shapes=[
            vm((VOC, D), BF), vm((16, QW), BF), vm((NX, 16, QW), BF), vm((GRP, D), BF),
            vm((8, 128), I32), vm((64, 8, 128), I32), vm((3, GRP, DS), BF),
            vm((GRP, VOC), F32), vm((GRP, VOC), F32), vm((GRP, VOC), F32),
            vm((8, GRP), F32), vm((8, 8, GRP), F32), vm((8, 8, GRP), F32), vm((GRP, 128), F32),
            vm((4, GRP, VOC), BF), vm((GRP, VOC), BF), vm((2, GRP, QW), F32),
            vm((Q, 128, QW), BF), vm((Q, 128, QW), BF), vm((Q, 128, QW), F32),
            vm((Q, 128, QW), BF), vm((Q, 3, 32, QW), BF),
            vm((Q, NZ, 16, 256), F32), vm((Q, NZ, 16, 256), BF), vm((Q, NZ - 1, 16, 256), BF),
            vm((DS, VOC), F32), vm((DS, VOC), BF),
            dma((5,)), dma((YC,)),
            dma((3,)), dma((3,)), dma((3,)), dma((3,)), dma((2, 4)), dma((2, 4)),
            dma((7,)), dma((7,)), dma((8,)), dma((8,)), dma, dma,
            dma((3,)), dma((3,)), dma((3,)), dma((3,)), dma((7,)), dma((7,)), dma((7,)), dma((7,)),
            dma((3, YC)), dma((3, YC)),
            dma((Q,)), dma((Q,)), dma((Q, 3)), dma((Q, 3)), dma((Q, 7)), dma((Q, 7)),
        ],
        compiler_params=pltpu.CompilerParams(
            collective_id=0, has_side_effects=True, vmem_limit_bytes=60 << 20
        ),
        cost_estimate=pl.CostEstimate(flops=8_100_000_000, bytes_accessed=14_000_000, transcendentals=330_000),
    )(hidden, head, row_weight, teacher_ids, teacher_probs)
    return row_grad, loss[:, 0], head_grad


def solution(mesh):
    in_specs = (
        P(("vocab", "rows"), None),
        P("vocab", None),
        P(("vocab", "rows")),
        P(("vocab", "rows"), None),
        P(("vocab", "rows"), None),
    )
    out_specs = (P(("vocab", "rows"), None), P(("vocab", "rows")), P("rows", "vocab"))
    return jax.shard_map(shards, mesh=mesh, in_specs=in_specs, out_specs=out_specs, check_vma=False)
```

```python
import jax
import jax.numpy as jnp
from jax import lax
from jax.experimental import pallas as pl
from jax.experimental.pallas import tpu as pltpu
from jax.sharding import PartitionSpec as P

MESH = pl.DeviceIdType.MESH
BF, F32, I32 = jnp.bfloat16, jnp.float32, jnp.int32
NZ, NX, NC, NY = 8, 4, 2, 4
D, VOC, TOPK = 4096, 1280, 128
GRP = 256
SLOTS = 16
DS = D // NY
Q = 4
QW = D // Q
DH = D // 2
PW = DH // 4
YC = 2
YW = VOC // YC


def iota(shape, dim):
    return lax.broadcasted_iota(I32, shape, dim)


def kernel(
    hidden, head_hbm, weight, ids, probs,
    row_out, loss_out, head_out,
    head, own_a, own_b, buf_a, buf_b, hid, meta_own, meta, hy,
    logits, e_buf, teacher, packet, st1, st2, cols, packet2, td1, td2, dot_buf,
    g_buf, gp, part, p_send, p_recv, s1, x_send, x_recv, z_f32, z_send, z_recv,
    acc, stage,
    sem_head, sem_out,
    xa_s, xa_r, zb_s, zb_r, xb_s, xb_r, xm_s, xm_r, ring_s, ring_r, zm_s, zm_r,
    sib_s, sib_r, sm_s, sm_r,
    hy_s, hy_r, hs_s, hs_r, st1_s, st1_r, st2_s, st2_r, td1_s, td1_r, td2_s, td2_r,
    y_s, y_r, f_s, f_r,
    rp_s, rp_r, rx_s, rx_r, rz_s, rz_r,
):
    v, y = lax.axis_index("vocab"), lax.axis_index("rows")
    z, x, c = lax.div(v, 8), lax.rem(lax.div(v, 2), 4), lax.rem(v, 2)
    oc = 1 - c

    def dev(dz=0, dx=0, dc=0, dy=0):
        zz = lax.rem(z + dz, NZ)
        xx = lax.rem(x + dx, NX)
        cc = c if dc == 0 else oc
        return (zz * 8 + xx * 2 + cc, lax.rem(y + dy, NY))

    started = []

    def send(src, dst, ss, rs, to):
        copy = pltpu.make_async_remote_copy(
            src_ref=src, dst_ref=dst, send_sem=ss, recv_sem=rs, device_id=to, device_id_type=MESH
        )
        copy.start()
        started.append(copy)
        return copy

    head_in = []
    for i in range(5):
        part_rows = pl.ds(i * 256, 256)
        copy = pltpu.make_async_copy(head_hbm.at[part_rows], head.at[part_rows], sem_head.at[i])
        copy.start()
        head_in.append(copy)

    xc = [(dx, dc) for dx in range(NX) for dc in range(NC) if (dx, dc) != (0, 0)]
    barrier = pltpu.get_barrier_semaphore()
    peers = [dev(dx=dx, dc=dc) for dx, dc in xc]
    peers += [dev(dz=d) for d in range(1, NZ)]
    peers += [dev(dy=d) for d in range(1, NY)]
    for to in peers:
        pl.semaphore_signal(barrier, inc=1, device_id=to, device_id_type=MESH)

    h = hidden[...].astype(F32)
    for own, at in ((own_a, 0), (own_b, DH)):
        own[...] = jnp.concatenate(
            [h[:, at + i * PW:at + (i + 1) * PW] for i in range(4)], axis=0
        ).astype(BF)
    meta_own[0:4, :] = ids[...]
    meta_own[4:8, :] = probs[...]
    pl.semaphore_wait(barrier, len(peers))

    got_a = [send(own_a, buf_a.at[x], xa_s.at[d - 1], xa_r.at[d - 1], dev(dx=d)) for d in (1, 3, 2)]
    got_b = [send(own_b, buf_b.at[x, z], zb_s.at[d - 1], zb_r.at[d - 1], dev(dz=d)) for d in range(1, NZ)]
    base = c * 8 + z
    blk = base * 4 + x
    got_m = [send(meta_own, meta.at[blk], xm_s.at[d - 1], xm_r.at[d - 1], dev(dx=d)) for d in (1, 3, 2)]
    buf_a[x] = own_a[...]
    buf_b[x, z] = own_b[...]
    meta[blk] = meta_own[...]

    def rows_of(zz):
        return pl.ds(pl.multiple_of((c * 8 + zz) * 16, 16), 16)

    def lay_out(blocks, zz, at):
        blocks = [b.astype(F32) for b in blocks]
        for i in range(4):
            hid[rows_of(zz), at + i * PW:at + (i + 1) * PW] = jnp.concatenate(
                [b[4 * i:4 * i + 4] for b in blocks], axis=0
            ).astype(BF)

    sib = []

    def sib_send(zz, at):
        ref, n = hid.at[rows_of(zz), at:at + DH], len(sib)
        sib.append(send(ref, ref, sib_s.at[n], sib_r.at[n], dev(dc=1)))

    def ring_send(way, step):
        zz = lax.rem(z + (NZ - step if way == 0 else step), NZ)
        ref = hid.at[rows_of(zz), 0:DH]
        return send(ref, ref, ring_s.at[way, step], ring_r.at[way, step], dev(dz=1 if way == 0 else NZ - 1))

    for copy in got_a:
        copy.wait_recv()
    lay_out([buf_a[i] for i in range(NX)], z, 0)
    now = [ring_send(0, 0), ring_send(1, 0)]
    sib_send(z, 0)
    for copy in got_m:
        copy.wait_recv()
    own_meta = meta.at[pl.ds((c * 8 + z) * 4, 4)]
    for step in range(1, 5):
        for way in range(2):
            if way == 1 and step == 4:
                continue
            now[way].wait_recv()
            if step < (4 if way == 0 else 3):
                now[way] = ring_send(way, step)
            sib_send(lax.rem(z + (NZ - step if way == 0 else step), NZ), 0)
        if step == 1:
            for copy in got_b:
                copy.wait_recv()
            mine = buf_b.at[x]
            got_b = [send(mine, mine, xb_s.at[d - 1], xb_r.at[d - 1], dev(dx=d)) for d in (1, 3, 2)]
            got_m = [
                send(own_meta, own_meta, zm_s.at[d - 1], zm_r.at[d - 1], dev(dz=d)) for d in range(1, NZ)
            ]
    for copy in got_b:
        copy.wait_recv()
    for zz in range(NZ):
        lay_out([buf_b[i, zz] for i in range(NX)], zz, DH)
        sib_send(zz, DH)

    half = pl.ds(pl.multiple_of(c * 128, 128), 128)
    got_hy = {}
    for d in (1, 3, 2):
        yy = lax.rem(y + d, NY)
        src = hid.at[half, pl.ds(pl.multiple_of(yy * DS, DS), DS)]
        got_hy[d] = send(src, hy.at[d - 1, half], hy_s.at[d - 1], hy_r.at[d - 1], dev(dy=d))

    for copy in got_m:
        copy.wait_recv()
    half_meta = meta.at[pl.ds(c * 32, 32)]
    got_sm = send(half_meta, half_meta, sm_s, sm_r, dev(dc=1))

    for copy in head_in:
        copy.wait()
    for copy in sib[:8]:
        copy.wait_recv()
    for n in range(5):
        ns = slice(n * 256, (n + 1) * 256)
        logits[:, ns] = lax.dot_general(
            hid[:, 0:DH], head[ns, 0:DH], (((1,), (1,)), ((), ())), preferred_element_type=F32
        )
    for copy in sib[8:]:
        copy.wait_recv()
    for n in range(5):
        ns = slice(n * 256, (n + 1) * 256)
        logits[:, ns] += lax.dot_general(
            hid[:, DH:D], head[ns, DH:D], (((1,), (1,)), ((), ())), preferred_element_type=F32
        )
    lg = logits[...]
    m_own = jnp.max(lg, axis=1, keepdims=True)
    ex = jnp.exp(lg - m_own)
    e_buf[...] = ex
    s_own = jnp.sum(ex, axis=1, keepdims=True)
    my_row = blk * 4
    row_id = iota((GRP, 128), 0)
    lane = iota((GRP, 128), 1)
    w_own = jnp.zeros((GRP, 128), F32)
    for r in range(4):
        w_own = jnp.where(row_id == my_row + r, weight[r], w_own)
    wide = jnp.where(lane == 0, m_own, jnp.where(lane == 1, s_own, w_own))
    packet[...] = wide.T[0:8, :]

    def combine(buf):
        top = buf[0, 0:1, :]
        for i in range(1, 8):
            top = jnp.maximum(top, buf[i, 0:1, :])
        total = [jnp.zeros((1, GRP), F32) for _ in range(2)]
        for i in range(8):
            total[0] = total[0] + buf[i, 1:2, :] * jnp.exp(buf[i, 0:1, :] - top)
            total[1] = total[1] + buf[i, 2:3, :]
        sub = iota((8, GRP), 0)
        return jnp.where(sub == 0, top, jnp.where(sub == 1, total[0], total[1]))

    place = x * 2 + c

    def over_xc(own, buf, ss, rs):
        got = [
            send(own, buf.at[place], ss.at[i], rs.at[i], dev(dx=dx, dc=dc))
            for i, (dx, dc) in enumerate(xc)
        ]
        buf[place] = own[...]
        return got

    def over_z(buf, ss, rs):
        mid = buf.at[z]
        return [send(mid, mid, ss.at[d - 1], rs.at[d - 1], dev(dz=d)) for d in range(1, NZ)]

    got = over_xc(packet, st1, st1_s, st1_r)
    got_sm.wait_recv()

    first = v * VOC
    all_meta = meta[...]
    off = all_meta[:, 0:4, :].reshape(GRP, TOPK) - first
    prob = all_meta[:, 4:8, :].reshape(GRP, TOPK)
    mine = jnp.logical_and(off >= 0, off < VOC)
    mask = jnp.where(mine, 1.0, 0.0).astype(BF)
    before = jnp.where(iota((TOPK, TOPK), 0) < iota((TOPK, TOPK), 1), 1.0, 0.0).astype(BF)
    ri, rj = iota((GRP, GRP), 0), iota((GRP, GRP), 1)
    earlier = jnp.where(jnp.logical_and((ri >> 2) == (rj >> 2), rj < ri), 1.0, 0.0).astype(BF)
    count = jnp.dot(mask, jnp.ones((TOPK, TOPK), BF), preferred_element_type=F32).astype(BF)
    rank = jnp.dot(mask, before, preferred_element_type=F32)
    rank = rank + jnp.dot(earlier, count, preferred_element_type=F32)
    rank = jnp.where(mine, rank, -1.0).reshape(64, 4, TOPK)
    rows4 = iota((GRP, TOPK), 0) & 3
    code = (off * 4 + rows4).astype(F32).reshape(64, 4, TOPK)
    probf = prob.astype(F32).reshape(64, 4, TOPK)
    slot = iota((64, SLOTS, TOPK), 1).astype(F32)
    code_at = jnp.zeros((64, SLOTS, TOPK), F32)
    prob_at = jnp.zeros((64, SLOTS, TOPK), F32)
    for r in range(4):
        hit = rank[:, r:r + 1, :] == slot
        code_at = code_at + jnp.where(hit, code[:, r:r + 1, :], 0.0)
        prob_at = prob_at + jnp.where(hit, probf[:, r:r + 1, :], 0.0)
    for copy in got:
        copy.wait_recv()
    st2[z] = combine(st1)
    got = over_z(st2, st2_s, st2_r)
    code_i = jnp.sum(code_at, axis=2, keepdims=True).reshape(64 * SLOTS, 1).astype(I32)
    prob_i = jnp.sum(prob_at, axis=2, keepdims=True).reshape(64 * SLOTS, 1).astype(I32)
    lanes = iota((256, 128), 1)
    places = iota((256, VOC), 1)
    block_row = (iota((256, 128), 0) >> 4) << 2
    for b in range(4):
        code_b, prob_b = code_i[b * 256:(b + 1) * 256], prob_i[b * 256:(b + 1) * 256]
        one_hot = jnp.where((code_b >> 2) == places, 1.0, 0.0).astype(BF)
        byte = jnp.where(lanes < 64, prob_b >> 8, prob_b & 255).astype(F32)
        at = jnp.where((lanes & 63) == block_row + (code_b & 3), byte, 0.0).astype(BF)
        both = lax.dot_general(at, one_hot, (((0,), (0,)), ((), ())), preferred_element_type=F32)
        teacher[b * 64:(b + 1) * 64, :] = (both[0:64] * 256.0 + both[64:128]) * (1.0 / 65536.0)

    t_own = jnp.sum(teacher[...] * logits[...], axis=1, keepdims=True)
    packet2[...] = jnp.broadcast_to(t_own, (GRP, 128)).T[0:8, :]
    for copy in got:
        copy.wait_recv()
    final = combine(st2)
    cols[...] = jnp.concatenate([final, jnp.zeros((120, GRP), F32)], axis=0).T
    top_c, total_c, w_c = cols[:, 0:1], cols[:, 1:2], cols[:, 2:3]
    scale = jnp.exp(m_own - top_c) / total_c
    g_buf[0] = (w_c * (e_buf[...] * scale - teacher[...])).astype(BF)

    got_y = {}
    for k in range(YC):
        ks = pl.ds(k * YW, YW)
        for d in (1, 3):
            got_y[d, k] = [send(
                g_buf.at[0, :, ks], g_buf.at[d, :, ks], y_s.at[d - 1, k], y_r.at[d - 1, k], dev(dy=d)
            )]

    def forward(k):
        ks = pl.ds(k * YW, YW)
        got_y[2, k] = []
        for d, n in ((1, 0), (3, 1)):
            got_y[d, k].pop().wait_recv()
            rows = pl.ds(n * 128, 128)
            got_y[2, k].append(send(
                g_buf.at[d, rows, ks], g_buf.at[2, rows, ks], f_s.at[n, k], f_r.at[n, k], dev(dy=d)
            ))

    got = over_xc(packet2, td1, td1_s, td1_r)

    i0 = iota((GRP, GRP), 0)
    src = ((i0 >> 7) << 7) + (((i0 >> 2) & 7) << 4) + (((i0 >> 5) & 3) << 2) + (i0 & 3)
    perm = jnp.where(src == iota((GRP, GRP), 1), 1.0, 0.0).astype(BF)
    gp[...] = jnp.dot(perm, g_buf[0], preferred_element_type=F32).astype(BF)
    other = pl.ds(pl.multiple_of(oc * 128, 128), 128)
    got_p, got_x, got_z = {}, {}, {}

    def pair_stage(q):
        part[q % 2] = jnp.dot(gp[...], head[:, q * QW:(q + 1) * QW], preferred_element_type=F32)
        p_send[q] = part[q % 2, other, :].astype(BF)
        got_p[q] = send(p_send.at[q], p_recv.at[q], rp_s.at[q], rp_r.at[q], dev(dc=1))

    def x_stage(q):
        got_p[q].wait_recv()
        s1[q] = part[q % 2, half, :] + p_recv[q].astype(F32)
        x_send[q] = s1[q].astype(BF)
        for d in (1, 3, 2):
            xx = lax.rem(x + d, NX)
            rows = pl.ds(pl.multiple_of(xx * 32, 32), 32)
            got_x[q, d] = send(
                x_send.at[q, rows], x_recv.at[q, d - 1], rx_s.at[q, d - 1], rx_r.at[q, d - 1], dev(dx=d)
            )

    def z_stage(q):
        for d in (1, 3, 2):
            got_x[q, d].wait_recv()
        s2 = s1[q, pl.ds(pl.multiple_of(x * 32, 32), 32), :]
        for d in range(3):
            s2 = s2 + x_recv[q, d].astype(F32)
        for zz in range(NZ):
            piece = jnp.concatenate([s2[4 * zz:4 * zz + 4, i * 256:(i + 1) * 256] for i in range(4)], axis=0)
            z_f32[q, zz] = piece
            z_send[q, zz] = piece.astype(BF)
        for d in range(1, NZ):
            zz = lax.rem(z + d, NZ)
            got_z[q, d] = send(
                z_send.at[q, zz], z_recv.at[q, d - 1], rz_s.at[q, d - 1], rz_r.at[q, d - 1], dev(dz=d)
            )

    def last_stage(q):
        for d in range(1, NZ):
            got_z[q, d].wait_recv()
        total = z_f32[q, z]
        for d in range(NZ - 1):
            total = total + z_recv[q, d].astype(F32)
        row_out[:, q * QW:(q + 1) * QW] = jnp.concatenate(
            [total[4 * i:4 * i + 4] for i in range(4)], axis=1
        ).astype(BF)

    def head_step(d, k):
        ks = slice(k * YW, (k + 1) * YW)
        if d == 0:
            left = hid[:, pl.ds(pl.multiple_of(y * DS, DS), DS)]
        else:
            left = hy[d - 1]
            for copy in got_y[d, k]:
                copy.wait_recv()
        term = lax.dot_general(
            left, g_buf[d, :, ks], (((0,), (0,)), ((), ())), preferred_element_type=F32
        )
        if d == 0:
            acc[:, ks] = term
        elif d != 2:
            acc[:, ks] += term
        else:
            stage[:, ks] = (acc[:, ks] + term).astype(BF)

    pair_stage(0)
    pair_stage(1)
    x_stage(0)
    pair_stage(2)
    x_stage(1)
    pair_stage(3)
    x_stage(2)
    x_stage(3)
    forward(0)
    for copy in got:
        copy.wait_recv()
    td2[z] = jnp.sum(td1[...], axis=0)
    got = over_z(td2, td2_s, td2_r)
    got_hs = []
    for d in (1, 3, 2):
        got_hy[d].wait_recv()
        ref = hy.at[d - 1, half]
        got_hs.append(send(ref, ref, hs_s.at[d - 1], hs_r.at[d - 1], dev(dc=1)))
    z_stage(0)
    z_stage(1)
    head_step(0, 0)
    forward(1)
    z_stage(2)
    head_step(0, 1)
    z_stage(3)
    for copy in got_hs:
        copy.wait_recv()
    for d in (1, 3):
        for k in range(YC):
            head_step(d, k)
    for q in range(Q):
        last_stage(q)
    for copy in got:
        copy.wait_recv()
    dots = jnp.concatenate([jnp.sum(td2[...], axis=0), jnp.zeros((120, GRP), F32)], axis=0).T
    dot_buf[...] = dots
    mine = pl.ds(pl.multiple_of(my_row, 4), 4)
    own_cols = cols[mine, :]
    own_loss = own_cols[:, 0:1] + jnp.log(own_cols[:, 1:2]) - dot_buf[mine, :][:, 0:1]
    at_lane = iota((4, 128), 0) == iota((4, 128), 1)
    loss_out[...] = jnp.sum(jnp.where(at_lane, own_loss, 0.0), axis=0, keepdims=True)
    outs = []
    for k in range(YC):
        head_step(2, k)
        ks = pl.ds(k * YW, YW)
        copy = pltpu.make_async_copy(stage.at[:, ks], head_out.at[:, ks], sem_out.at[k])
        copy.start()
        outs.append(copy)
    for copy in started:
        copy.wait_send()
    for copy in outs:
        copy.wait()


def hand_out(row, loss, head, row_out, loss_out, head_out, buf, sem_in, sem_out):
    parts = [pl.ds(i * (DS // 8), DS // 8) for i in range(8)]
    ins = [pltpu.make_async_copy(head.at[p], buf.at[p], sem_in.at[i]) for i, p in enumerate(parts)]
    outs = [pltpu.make_async_copy(buf.at[p], head_out.at[p], sem_out.at[i]) for i, p in enumerate(parts)]
    for copy in ins:
        copy.start()
    row_out[...] = row[...]
    loss_out[...] = loss[0, 0:4]
    for arrive, leave in zip(ins, outs):
        arrive.wait()
        leave.start()
    for copy in outs:
        copy.wait()


def shards(hidden, head, row_weight, teacher_ids, teacher_probs):
    dma = pltpu.SemaphoreType.DMA
    vm = pltpu.VMEM
    any_spec = pl.BlockSpec(memory_space=pl.ANY)
    vm_spec = pl.BlockSpec(memory_space=pltpu.VMEM)
    row_grad, loss, head_grad = pl.pallas_call(
        kernel,
        out_shape=(
            jax.ShapeDtypeStruct((4, D), BF),
            jax.ShapeDtypeStruct((1, 128), F32),
            jax.ShapeDtypeStruct((DS, VOC), BF),
        ),
        in_specs=[vm_spec, any_spec, pl.BlockSpec(memory_space=pltpu.SMEM), vm_spec, vm_spec],
        out_specs=(vm_spec, vm_spec, any_spec),
        scratch_shapes=[
            vm((VOC, D), BF), vm((16, PW), BF), vm((16, PW), BF),
            vm((NX, 16, PW), BF), vm((NX, NZ, 16, PW), BF), vm((GRP, D), BF),
            vm((8, 128), I32), vm((64, 8, 128), I32), vm((3, GRP, DS), BF),
            vm((GRP, VOC), F32), vm((GRP, VOC), F32), vm((GRP, VOC), F32),
            vm((8, GRP), F32), vm((8, 8, GRP), F32), vm((8, 8, GRP), F32), vm((GRP, 128), F32),
            vm((8, GRP), F32), vm((8, 8, GRP), F32), vm((8, 8, GRP), F32), vm((GRP, 128), F32),
            vm((4, GRP, VOC), BF), vm((GRP, VOC), BF), vm((2, GRP, QW), F32),
            vm((Q, 128, QW), BF), vm((Q, 128, QW), BF), vm((Q, 128, QW), F32),
            vm((Q, 128, QW), BF), vm((Q, 3, 32, QW), BF),
            vm((Q, NZ, 16, 256), F32), vm((Q, NZ, 16, 256), BF), vm((Q, NZ - 1, 16, 256), BF),
            vm((DS, VOC), F32), vm((DS, VOC), BF),
            dma((5,)), dma((YC,)),
            dma((3,)), dma((3,)), dma((7,)), dma((7,)), dma((3,)), dma((3,)), dma((3,)), dma((3,)),
            dma((2, 4)), dma((2, 4)), dma((7,)), dma((7,)), dma((16,)), dma((16,)), dma, dma,
            dma((3,)), dma((3,)), dma((3,)), dma((3,)), dma((7,)), dma((7,)), dma((7,)), dma((7,)),
            dma((7,)), dma((7,)), dma((7,)), dma((7,)),
            dma((3, YC)), dma((3, YC)), dma((2, YC)), dma((2, YC)),
            dma((Q,)), dma((Q,)), dma((Q, 3)), dma((Q, 3)), dma((Q, 7)), dma((Q, 7)),
        ],
        compiler_params=pltpu.CompilerParams(
            collective_id=0, has_side_effects=True, vmem_limit_bytes=60 << 20
        ),
        cost_estimate=pl.CostEstimate(flops=8_100_000_000, bytes_accessed=14_000_000, transcendentals=330_000),
    )(hidden, head, row_weight, teacher_ids, teacher_probs)
    return pl.pallas_call(
        hand_out,
        out_shape=(
            jax.ShapeDtypeStruct((4, D), BF),
            jax.ShapeDtypeStruct((4,), F32),
            jax.ShapeDtypeStruct((DS, VOC), BF),
        ),
        in_specs=[vm_spec, vm_spec, any_spec],
        out_specs=(vm_spec, vm_spec, any_spec),
        scratch_shapes=[vm((DS, VOC), BF), dma((8,)), dma((8,))],
    )(row_grad, loss, head_grad)


def solution(mesh):
    in_specs = (
        P(("vocab", "rows"), None),
        P("vocab", None),
        P(("vocab", "rows")),
        P(("vocab", "rows"), None),
        P(("vocab", "rows"), None),
    )
    out_specs = (P(("vocab", "rows"), None), P(("vocab", "rows")), P("rows", "vocab"))
    return jax.shard_map(shards, mesh=mesh, in_specs=in_specs, out_specs=out_specs, check_vma=False)
```

```python
import jax
import jax.numpy as jnp
from jax import lax
from jax.experimental import pallas as pl
from jax.experimental.pallas import tpu as pltpu
from jax.sharding import PartitionSpec as P

MESH = pl.DeviceIdType.MESH
BF, F32, I32 = jnp.bfloat16, jnp.float32, jnp.int32
NZ, NX, NC, NY = 8, 4, 2, 4
D, VOC, TOPK = 4096, 1280, 128
GRP = 256
SLOTS = 16
DS = D // NY
CHUNKS = ((0, 1536), (1536, 1024), (2560, 1024), (3584, 512))
NQ = len(CHUNKS)
DH = D // 2
PW = DH // 4
RING = 1
RW = DH // RING
HW = DS // 4
YC = 2
YW = VOC // YC


def iota(shape, dim):
    return lax.broadcasted_iota(I32, shape, dim)


def kernel(
    hidden, head_hbm, weight, ids, probs,
    row_out, loss_out, head_out,
    head, own_a, own_b, own_h, buf_a, buf_b, buf_h, hid, meta_own, meta, hy,
    logits, teacher, lists, packet, st1, st2, cols, packet2, td1, td2, dot_buf, scales, scale_c,
    e_buf, grad, ep, tp, part1, part2, p1_send, p1_recv, p2_send, p2_recv,
    s1, x_send, x_recv, z_f32, z_send, z_recv,
    acc,
    sem_head,
    xa_s, xa_r, zb_s, zb_r, xb_s, xb_r, yh_s, yh_r, zh_s, zh_r, xh_s, xh_r, xm_s, xm_r, ring_s, ring_r, zm_s, zm_r,
    sib_s, sib_r, sm_s, sm_r,
    hs_s, hs_r, st1_s, st1_r, st2_s, st2_r, td1_s, td1_r, td2_s, td2_r,
    y_s, y_r, f_s, f_r, l_s, l_r, sc_s, sc_r,
    p1_s, p1_r, p2_s, p2_r, rx_s, rx_r, rz_s, rz_r,
):
    v, y = lax.axis_index("vocab"), lax.axis_index("rows")
    z, x, c = lax.div(v, 8), lax.rem(lax.div(v, 2), 4), lax.rem(v, 2)
    oc = 1 - c

    def dev(dz=0, dx=0, dc=0, dy=0):
        zz = lax.rem(z + dz, NZ)
        xx = lax.rem(x + dx, NX)
        cc = c if dc == 0 else oc
        return (zz * 8 + xx * 2 + cc, lax.rem(y + dy, NY))

    started = []

    def send(src, dst, ss, rs, to):
        copy = pltpu.make_async_remote_copy(
            src_ref=src, dst_ref=dst, send_sem=ss, recv_sem=rs, device_id=to, device_id_type=MESH
        )
        copy.start()
        started.append(copy)
        return copy

    head_in = []
    for i in range(5):
        part_rows = pl.ds(i * 256, 256)
        copy = pltpu.make_async_copy(head_hbm.at[part_rows], head.at[part_rows], sem_head.at[i])
        copy.start()
        head_in.append(copy)

    xc = [(dx, dc) for dx in range(NX) for dc in range(NC) if (dx, dc) != (0, 0)]
    barrier = pltpu.get_barrier_semaphore()
    peers = [dev(dx=dx, dc=dc) for dx, dc in xc]
    peers += [dev(dz=d) for d in range(1, NZ)]
    peers += [dev(dy=d) for d in range(1, NY)]
    for to in peers:
        pl.semaphore_signal(barrier, inc=1, device_id=to, device_id_type=MESH)

    h = hidden[...].astype(F32)
    for own, at in ((own_a, 0), (own_b, DH)):
        own[...] = jnp.concatenate(
            [h[:, at + i * PW:at + (i + 1) * PW] for i in range(4)], axis=0
        ).astype(BF)
    for d in (1, 3, 2):
        yy = lax.rem(y + d, NY)
        hs = hidden[:, pl.ds(pl.multiple_of(yy * DS, DS), DS)].astype(F32)
        own_h[d - 1] = jnp.concatenate([hs[:, i * HW:(i + 1) * HW] for i in range(4)], axis=0).astype(BF)
    meta_own[0:4, :] = ids[...]
    meta_own[4:8, :] = probs[...]
    pl.semaphore_wait(barrier, len(peers))

    got_a = [send(own_a, buf_a.at[x], xa_s.at[d - 1], xa_r.at[d - 1], dev(dx=d)) for d in (1, 3, 2)]
    got_b = [send(own_b, buf_b.at[x, z], zb_s.at[d - 1], zb_r.at[d - 1], dev(dz=d)) for d in range(1, NZ)]
    base = c * 8 + z
    blk = base * 4 + x
    got_m = [send(meta_own, meta.at[blk], xm_s.at[d - 1], xm_r.at[d - 1], dev(dx=d)) for d in (1, 3, 2)]
    got_h = [
        send(own_h.at[d - 1], buf_h.at[x, z, d - 1], yh_s.at[d - 1], yh_r.at[d - 1], dev(dy=d)) for d in (1, 3, 2)
    ]
    buf_a[x] = own_a[...]
    buf_b[x, z] = own_b[...]
    meta[blk] = meta_own[...]

    def rows_of(zz):
        return pl.ds(pl.multiple_of((c * 8 + zz) * 16, 16), 16)

    def lay_out(blocks, zz, at):
        blocks = [b.astype(F32) for b in blocks]
        for i in range(4):
            hid[rows_of(zz), at + i * PW:at + (i + 1) * PW] = jnp.concatenate(
                [b[4 * i:4 * i + 4] for b in blocks], axis=0
            ).astype(BF)

    sib = []

    def sib_send(zz, at):
        ref, n = hid.at[rows_of(zz), at:at + DH], len(sib)
        sib.append(send(ref, ref, sib_s.at[n], sib_r.at[n], dev(dc=1)))

    def ring_send(way, step):
        zz = lax.rem(z + (NZ - step if way == 0 else step), NZ)
        sent = []
        for n in range(RING):
            ref = hid.at[rows_of(zz), n * RW:(n + 1) * RW]
            sent.append(send(
                ref, ref, ring_s.at[way, step, n], ring_r.at[way, step, n], dev(dz=1 if way == 0 else NZ - 1)
            ))
        return sent

    got_xb = []

    def block_send(dz):
        zz = lax.rem(z + NZ - dz, NZ)
        if dz:
            got_b[dz - 1].wait_recv()
        ref = buf_b.at[x, zz]
        for d in (1, 3, 2):
            got_xb.append(send(ref, ref, xb_s.at[dz, d - 1], xb_r.at[dz, d - 1], dev(dx=d)))

    for copy in got_a:
        copy.wait_recv()
    lay_out([buf_a[i] for i in range(NX)], z, 0)
    now = [ring_send(0, 0), ring_send(1, 0)]
    sib_send(z, 0)
    for copy in got_m:
        copy.wait_recv()
    own_meta = meta.at[pl.ds((c * 8 + z) * 4, 4)]
    got_m = [send(own_meta, own_meta, zm_s.at[d - 1], zm_r.at[d - 1], dev(dz=d)) for d in range(1, NZ)]
    for step in range(1, 5):
        for way in range(2):
            if way == 1 and step == 4:
                continue
            for copy in now[way]:
                copy.wait_recv()
            if step < (4 if way == 0 else 3):
                now[way] = ring_send(way, step)
            sib_send(lax.rem(z + (NZ - step if way == 0 else step), NZ), 0)
        if step == 1:
            for copy in got_b:
                copy.wait_recv()
            mine = buf_b.at[x]
            for d in (1, 3, 2):
                got_xb.append(send(mine, mine, xb_s.at[0, d - 1], xb_r.at[0, d - 1], dev(dx=d)))
        if step == 2:
            for copy in got_h:
                copy.wait_recv()
            mine = buf_h.at[x, z]
            got_h = [send(mine, mine, zh_s.at[d - 1], zh_r.at[d - 1], dev(dz=d)) for d in range(1, NZ)]
    for copy in got_h:
        copy.wait_recv()
    mine = buf_h.at[x]
    got_h = [send(mine, mine, xh_s.at[d - 1], xh_r.at[d - 1], dev(dx=d)) for d in (1, 3, 2)]
    for copy in got_m:
        copy.wait_recv()
    half_meta = meta.at[pl.ds(c * 32, 32)]
    send(half_meta, half_meta, sm_s, sm_r, dev(dc=1)).wait_recv()

    for copy in got_xb:
        copy.wait_recv()
    for zz in range(NZ):
        lay_out([buf_b[i, zz] for i in range(NX)], zz, DH)
        sib_send(zz, DH)

    half = pl.ds(pl.multiple_of(c * 128, 128), 128)

    for copy in head_in:
        copy.wait()
    for copy in sib[:8]:
        copy.wait_recv()
    for n in range(5):
        ns = slice(n * 256, (n + 1) * 256)
        logits[:, ns] = lax.dot_general(
            hid[:, 0:DH], head[ns, 0:DH], (((1,), (1,)), ((), ())), preferred_element_type=F32
        )
    for copy in sib[8:]:
        copy.wait_recv()
    for n in range(5):
        ns = slice(n * 256, (n + 1) * 256)
        logits[:, ns] += lax.dot_general(
            hid[:, DH:D], head[ns, DH:D], (((1,), (1,)), ((), ())), preferred_element_type=F32
        )
    lg = logits[...]
    m_own = jnp.max(lg, axis=1, keepdims=True)
    ex = jnp.exp(lg - m_own)
    e_buf[0] = ex.astype(BF)
    s_own = jnp.sum(ex, axis=1, keepdims=True)
    my_row = blk * 4
    row_id = iota((GRP, 128), 0)
    lane = iota((GRP, 128), 1)
    w_own = jnp.zeros((GRP, 128), F32)
    for r in range(4):
        w_own = jnp.where(row_id == my_row + r, weight[r], w_own)
    wide = jnp.where(lane == 0, m_own, jnp.where(lane == 1, s_own, w_own))
    packet[...] = wide.T[0:8, :]

    def combine(buf):
        top = buf[0, 0:1, :]
        for i in range(1, 8):
            top = jnp.maximum(top, buf[i, 0:1, :])
        total = [jnp.zeros((1, GRP), F32) for _ in range(2)]
        for i in range(8):
            total[0] = total[0] + buf[i, 1:2, :] * jnp.exp(buf[i, 0:1, :] - top)
            total[1] = total[1] + buf[i, 2:3, :]
        sub = iota((8, GRP), 0)
        return jnp.where(sub == 0, top, jnp.where(sub == 1, total[0], total[1]))

    place = x * 2 + c

    def over_xc(own, buf, ss, rs):
        got = [
            send(own, buf.at[place], ss.at[i], rs.at[i], dev(dx=dx, dc=dc))
            for i, (dx, dc) in enumerate(xc)
        ]
        buf[place] = own[...]
        return got

    def over_z(buf, ss, rs):
        mid = buf.at[z]
        return [send(mid, mid, ss.at[d - 1], rs.at[d - 1], dev(dz=d)) for d in range(1, NZ)]

    got = over_xc(packet, st1, st1_s, st1_r)

    got_y = {}
    for k in range(YC):
        ks = pl.ds(k * YW, YW)
        for d in (1, 3):
            got_y[d, k] = [send(
                e_buf.at[0, :, ks], e_buf.at[d, :, ks], y_s.at[d - 1, k], y_r.at[d - 1, k], dev(dy=d)
            )]

    def forward(k):
        ks = pl.ds(k * YW, YW)
        got_y[2, k] = []
        for d, n in ((1, 0), (3, 1)):
            got_y[d, k].pop().wait_recv()
            rows = pl.ds(n * 128, 128)
            got_y[2, k].append(send(
                e_buf.at[d, rows, ks], e_buf.at[2, rows, ks], f_s.at[n, k], f_r.at[n, k], dev(dy=d)
            ))

    i0 = iota((GRP, GRP), 0)
    src = ((i0 >> 7) << 7) + (((i0 >> 2) & 7) << 4) + (((i0 >> 5) & 3) << 2) + (i0 & 3)
    perm = jnp.where(src == iota((GRP, GRP), 1), 1.0, 0.0).astype(BF)
    other = pl.ds(pl.multiple_of(oc * 128, 128), 128)
    got_p1, got_x, got_z = {}, {}, {}

    def pair_send(q, part, p_send, p_recv, ss, rs, left):
        at, width = CHUNKS[q]
        qs = slice(at, at + width)
        part[:, qs] = jnp.dot(left[...], head[:, qs], preferred_element_type=F32)
        p_send[:, qs] = part[other, qs].astype(BF)
        return send(p_send.at[:, qs], p_recv.at[:, qs], ss, rs, dev(dc=1))

    ep[...] = jnp.dot(perm, e_buf[0], preferred_element_type=F32).astype(BF)
    got_p1[0] = pair_send(0, part1, p1_send, p1_recv, p1_s.at[0], p1_r.at[0], ep)
    for copy in got:
        copy.wait_recv()
    st2[z] = combine(st1)
    got = over_z(st2, st2_s, st2_r)

    off = meta[:, 0:4, :].reshape(GRP, TOPK) - v * VOC
    prob = meta[:, 4:8, :].reshape(GRP, TOPK)
    mine = jnp.logical_and(off >= 0, off < VOC)
    mask = jnp.where(mine, 1.0, 0.0).astype(BF)
    before = jnp.where(iota((TOPK, TOPK), 0) < iota((TOPK, TOPK), 1), 1.0, 0.0).astype(BF)
    ri, rj = iota((GRP, GRP), 0), iota((GRP, GRP), 1)
    earlier = jnp.where(jnp.logical_and((ri >> 2) == (rj >> 2), rj < ri), 1.0, 0.0).astype(BF)
    count = jnp.dot(mask, jnp.ones((TOPK, TOPK), BF), preferred_element_type=F32).astype(BF)
    rank = jnp.dot(mask, before, preferred_element_type=F32)
    rank = rank + jnp.dot(earlier, count, preferred_element_type=F32)
    rank = jnp.where(mine, rank, -1.0).reshape(64, 4, TOPK)
    rows4 = iota((GRP, TOPK), 0) & 3
    code = (off * 4 + rows4).astype(F32).reshape(64, 4, TOPK)
    probf = prob.astype(F32).reshape(64, 4, TOPK)
    slot = iota((64, SLOTS, TOPK), 1)
    lane3 = iota((64, SLOTS, TOPK), 2)
    slot_f = slot.astype(F32)
    code_at = jnp.zeros((64, SLOTS, TOPK), F32)
    prob_at = jnp.zeros((64, SLOTS, TOPK), F32)
    for r in range(4):
        hit = rank[:, r:r + 1, :] == slot_f
        code_at = code_at + jnp.where(hit, code[:, r:r + 1, :], 0.0)
        prob_at = prob_at + jnp.where(hit, probf[:, r:r + 1, :], 0.0)
    code_c = jnp.sum(code_at, axis=2, keepdims=True)
    prob_c = jnp.sum(prob_at, axis=2, keepdims=True)
    lists[0] = jnp.sum(
        jnp.where(lane3 == slot, code_c, 0.0) + jnp.where(lane3 == slot + SLOTS, prob_c, 0.0), axis=1
    )
    got_l = {
        d: send(lists.at[0], lists.at[d], l_s.at[d - 1], l_r.at[d - 1], dev(dy=d)) for d in (1, 3, 2)
    }
    lanes = iota((256, 128), 1)
    places = iota((256, VOC), 1)
    block_row = (iota((256, 128), 0) >> 4) << 2

    def make_teacher(code_c, prob_c):
        code_i = code_c.reshape(64 * SLOTS, 1).astype(I32)
        prob_i = prob_c.reshape(64 * SLOTS, 1).astype(I32)
        for b in range(4):
            code_b, prob_b = code_i[b * 256:(b + 1) * 256], prob_i[b * 256:(b + 1) * 256]
            one_hot = jnp.where((code_b >> 2) == places, 1.0, 0.0).astype(BF)
            byte = jnp.where(lanes < 64, prob_b >> 8, prob_b & 255).astype(F32)
            at = jnp.where((lanes & 63) == block_row + (code_b & 3), byte, 0.0).astype(BF)
            both = lax.dot_general(at, one_hot, (((0,), (0,)), ((), ())), preferred_element_type=F32)
            teacher[b * 64:(b + 1) * 64, :] = (both[0:64] * 256.0 + both[64:128]) * (1.0 / 65536.0)

    def other_teacher(d):
        got_l[d].wait_recv()
        flat = jnp.broadcast_to(lists[d][:, None, :], (64, SLOTS, TOPK))
        make_teacher(
            jnp.sum(jnp.where(lane3 == slot, flat, 0.0), axis=2, keepdims=True),
            jnp.sum(jnp.where(lane3 == slot + SLOTS, flat, 0.0), axis=2, keepdims=True),
        )

    make_teacher(code_c, prob_c)
    tp[...] = jnp.dot(perm, teacher[...].astype(BF), preferred_element_type=F32).astype(BF)
    got_p2 = pair_send(0, part2, p2_send, p2_recv, p2_s, p2_r, tp)
    t_own = jnp.sum(teacher[...] * logits[...], axis=1, keepdims=True)
    packet2[...] = jnp.broadcast_to(t_own, (GRP, 128)).T[0:8, :]
    got_td = over_xc(packet2, td1, td1_s, td1_r)
    for copy in got:
        copy.wait_recv()

    final = combine(st2)
    top, ratio, w_row = final[0:1, :], final[2:3, :] / final[1:2, :], final[2:3, :]
    a_row = jnp.exp(packet[0:1, :] - top) * ratio
    b_row = jnp.exp(st1[x * 2 + oc, 0:1, :] - top) * ratio
    scales[0] = jnp.concatenate([a_row, w_row, b_row, final[0:2, :], jnp.zeros((3, GRP), F32)], axis=0)
    got_sc = {
        d: send(scales.at[0], scales.at[d], sc_s.at[d - 1], sc_r.at[d - 1], dev(dy=d)) for d in (1, 3, 2)
    }

    def columns(d):
        return jnp.concatenate([scales[d], jnp.zeros((120, GRP), F32)], axis=0).T

    cols[...] = columns(0)
    scale_c[...] = jnp.concatenate(
        [
            cols[i * 128 + k * 16 + j * 4:i * 128 + k * 16 + j * 4 + 4, :]
            for i in range(NC) for j in range(NX) for k in range(NZ)
        ],
        axis=0,
    )

    def x_stage(q):
        at, width = CHUNKS[q]
        qs = slice(at, at + width)
        got_p1[q].wait_recv()
        if q == 0:
            got_p2.wait_recv()
            sc = scale_c[half, :]
            total = sc[:, 0:1] * part1[half, qs] + sc[:, 2:3] * p1_recv[:, qs].astype(F32)
            total = total - sc[:, 1:2] * (part2[half, qs] + p2_recv[...].astype(F32))
        else:
            total = part1[half, qs] + p1_recv[:, qs].astype(F32)
        s1[:, qs] = total
        x_send[:, qs] = total.astype(BF)
        for d in (1, 3, 2):
            xx = lax.rem(x + d, NX)
            rows = pl.ds(pl.multiple_of(xx * 32, 32), 32)
            got_x[q, d] = send(
                x_send.at[rows, qs], x_recv.at[d - 1, :, qs], rx_s.at[q, d - 1], rx_r.at[q, d - 1], dev(dx=d)
            )

    def pair_stage(q):
        got_p1[q] = pair_send(q, part1, p1_send, p1_recv, p1_s.at[q], p1_r.at[q], ep)

    def z_stage(q):
        at, width = CHUNKS[q]
        qs = slice(at, at + width)
        w4 = width // 4
        zs = slice(at // 4, at // 4 + w4)
        for d in (1, 3, 2):
            got_x[q, d].wait_recv()
        s2 = s1[pl.ds(pl.multiple_of(x * 32, 32), 32), qs]
        for d in range(3):
            s2 = s2 + x_recv[d, :, qs].astype(F32)
        for zz in range(NZ):
            piece = jnp.concatenate([s2[4 * zz:4 * zz + 4, i * w4:(i + 1) * w4] for i in range(4)], axis=0)
            z_f32[zz, :, zs] = piece
            z_send[zz, :, zs] = piece.astype(BF)
        for d in range(1, NZ):
            zz = lax.rem(z + d, NZ)
            got_z[q, d] = send(
                z_send.at[zz, :, zs], z_recv.at[d - 1, :, zs], rz_s.at[q, d - 1], rz_r.at[q, d - 1], dev(dz=d)
            )

    def last_stage(q):
        at, width = CHUNKS[q]
        w4 = width // 4
        zs = slice(at // 4, at // 4 + w4)
        for d in range(1, NZ):
            got_z[q, d].wait_recv()
        total = z_f32[z, :, zs]
        for d in range(NZ - 1):
            total = total + z_recv[d, :, zs].astype(F32)
        row_out[:, at:at + width] = jnp.concatenate(
            [total[4 * i:4 * i + 4] for i in range(4)], axis=1
        ).astype(BF)

    def head_step(d, k):
        ks = slice(k * YW, (k + 1) * YW)
        if d == 0:
            left, sc = hid[:, pl.ds(pl.multiple_of(y * DS, DS), DS)], cols
        else:
            left, sc = hy[d - 1], scale_c
            for copy in got_y[d, k]:
                copy.wait_recv()
        grad[:, ks] = (sc[:, 0:1] * e_buf[d, :, ks].astype(F32) - sc[:, 1:2] * teacher[:, ks]).astype(BF)
        term = lax.dot_general(
            left, grad[:, ks], (((0,), (0,)), ((), ())), preferred_element_type=F32
        )
        if d == 0:
            acc[:, ks] = term
        elif d != 2:
            acc[:, ks] += term
        else:
            head_out[:, ks] = (acc[:, ks] + term).astype(BF)

    def prepare(d):
        other_teacher(d)
        got_sc[d].wait_recv()
        scale_c[...] = columns(d)

    x_stage(0)
    ep[...] = (scale_c[:, 0:1] * ep[...].astype(F32) - scale_c[:, 1:2] * tp[...].astype(F32)).astype(BF)
    pair_stage(1)
    pair_stage(2)
    x_stage(1)
    pair_stage(3)
    x_stage(2)
    x_stage(3)
    forward(0)
    for copy in got_h:
        copy.wait_recv()
    got_hs = []
    for d in (1, 3, 2):
        for zz in range(NZ):
            blocks = [buf_h[j, zz, d - 1].astype(F32) for j in range(NX)]
            for i in range(4):
                hy[d - 1, rows_of(zz), i * HW:(i + 1) * HW] = jnp.concatenate(
                    [b[4 * i:4 * i + 4] for b in blocks], axis=0
                ).astype(BF)
        ref = hy.at[d - 1, half]
        got_hs.append(send(ref, ref, hs_s.at[d - 1], hs_r.at[d - 1], dev(dc=1)))
    head_step(0, 0)
    head_step(0, 1)
    forward(1)
    for copy in got_td:
        copy.wait_recv()
    td2[z] = jnp.sum(td1[...], axis=0)
    got_td = over_z(td2, td2_s, td2_r)
    z_stage(0)
    for copy in got_hs:
        copy.wait_recv()
    prepare(1)
    head_step(1, 0)
    z_stage(1)
    head_step(1, 1)
    prepare(3)
    z_stage(2)
    head_step(3, 0)
    head_step(3, 1)
    z_stage(3)
    prepare(2)
    for k in range(YC):
        head_step(2, k)
    for q in range(NQ):
        last_stage(q)
    for copy in got_td:
        copy.wait_recv()
    dots = jnp.concatenate([jnp.sum(td2[...], axis=0), jnp.zeros((120, GRP), F32)], axis=0).T
    dot_buf[...] = dots
    mine = pl.ds(pl.multiple_of(my_row, 4), 4)
    own_cols = cols[mine, :]
    own_loss = own_cols[:, 3:4] + jnp.log(own_cols[:, 4:5]) - dot_buf[mine, :][:, 0:1]
    at_lane = iota((4, 128), 0) == iota((4, 128), 1)
    loss_out[...] = jnp.sum(jnp.where(at_lane, own_loss, 0.0), axis=0)[0:4]
    for copy in started:
        copy.wait_send()


def shards(hidden, head, row_weight, teacher_ids, teacher_probs):
    dma = pltpu.SemaphoreType.DMA
    vm = pltpu.VMEM
    any_spec = pl.BlockSpec(memory_space=pl.ANY)
    vm_spec = pl.BlockSpec(memory_space=pltpu.VMEM)
    return pl.pallas_call(
        kernel,
        out_shape=(
            vm((4, D), BF),
            vm((4,), F32),
            vm((DS, VOC), BF),
        ),
        in_specs=[vm_spec, any_spec, pl.BlockSpec(memory_space=pltpu.SMEM), vm_spec, vm_spec],
        out_specs=(vm_spec, vm_spec, vm_spec),
        scratch_shapes=[
            vm((VOC, D), BF), vm((16, PW), BF), vm((16, PW), BF), vm((3, 16, HW), BF),
            vm((NX, 16, PW), BF), vm((NX, NZ, 16, PW), BF), vm((NX, NZ, 3, 16, HW), BF), vm((GRP, D), BF),
            vm((8, 128), I32), vm((64, 8, 128), I32), vm((3, GRP, DS), BF),
            vm((GRP, VOC), F32), vm((GRP, VOC), F32), vm((4, 64, TOPK), F32),
            vm((8, GRP), F32), vm((8, 8, GRP), F32), vm((8, 8, GRP), F32), vm((GRP, 128), F32),
            vm((8, GRP), F32), vm((8, 8, GRP), F32), vm((8, 8, GRP), F32), vm((GRP, 128), F32),
            vm((4, 8, GRP), F32), vm((GRP, 128), F32),
            vm((4, GRP, VOC), BF), vm((GRP, VOC), BF), vm((GRP, VOC), BF), vm((GRP, VOC), BF),
            vm((GRP, D), F32), vm((GRP, CHUNKS[0][1]), F32),
            vm((128, D), BF), vm((128, D), BF), vm((128, CHUNKS[0][1]), BF), vm((128, CHUNKS[0][1]), BF),
            vm((128, D), F32), vm((128, D), BF), vm((3, 32, D), BF),
            vm((NZ, 16, D // 4), F32), vm((NZ, 16, D // 4), BF), vm((NZ - 1, 16, D // 4), BF),
            vm((DS, VOC), F32),
            dma((5,)),
            dma((3,)), dma((3,)), dma((7,)), dma((7,)), dma((1, 3)), dma((1, 3)),
            dma((3,)), dma((3,)), dma((7,)), dma((7,)), dma((3,)), dma((3,)), dma((3,)), dma((3,)),
            dma((2, 4, RING)), dma((2, 4, RING)), dma((7,)), dma((7,)), dma((16,)), dma((16,)), dma, dma,
            dma((3,)), dma((3,)), dma((7,)), dma((7,)), dma((7,)), dma((7,)),
            dma((7,)), dma((7,)), dma((7,)), dma((7,)),
            dma((3, YC)), dma((3, YC)), dma((2, YC)), dma((2, YC)),
            dma((3,)), dma((3,)), dma((3,)), dma((3,)),
            dma((NQ,)), dma((NQ,)), dma, dma, dma((NQ, 3)), dma((NQ, 3)), dma((NQ, 7)), dma((NQ, 7)),
        ],
        compiler_params=pltpu.CompilerParams(
            collective_id=0, has_side_effects=True, vmem_limit_bytes=52 << 20
        ),
        cost_estimate=pl.CostEstimate(flops=8_100_000_000, bytes_accessed=14_000_000, transcendentals=330_000),
    )(hidden, head, row_weight, teacher_ids, teacher_probs)


def solution(mesh):
    in_specs = (
        P(("vocab", "rows"), None),
        P("vocab", None),
        P(("vocab", "rows")),
        P(("vocab", "rows"), None),
        P(("vocab", "rows"), None),
    )
    out_specs = (P(("vocab", "rows"), None), P(("vocab", "rows")), P("rows", "vocab"))
    return jax.shard_map(shards, mesh=mesh, in_specs=in_specs, out_specs=out_specs, check_vma=False)
```

```python
import jax
import jax.numpy as jnp
from jax import lax
from jax.experimental import pallas as pl
from jax.experimental.pallas import tpu as pltpu
from jax.sharding import PartitionSpec as P

MESH = pl.DeviceIdType.MESH
BF, F32, I32 = jnp.bfloat16, jnp.float32, jnp.int32
NZ, NX, NC, NY = 8, 4, 2, 4
D, VOC, TOPK = 4096, 1280, 128
GRP = 256
SLOTS = 16
DS = D // NY
CHUNKS = ((0, 1536), (1536, 1024), (2560, 1024), (3584, 512))
NQ = len(CHUNKS)
DH = D // 2
PW = DH // 4
RING = 1
RW = DH // RING
HW = DS // 4
YCH = ((0, 768), (768, 512))
YC = len(YCH)


def iota(shape, dim):
    return lax.broadcasted_iota(I32, shape, dim)


def kernel(
    hidden, head_hbm, weight, ids, probs,
    row_out, loss_out, head_out,
    head, own_a, own_b, own_h, buf_a, buf_b, buf_h, hid, meta_own, meta, hy,
    logits, teacher, lists, packet, st1, st2, cols, packet2, td1, td2, dot_buf, scales, scale_c,
    e_buf, grad, ep, tp, part1, part2, p1_send, p1_recv, p2_send, p2_recv,
    s1, x_send, x_recv, z_f32, z_send, z_recv,
    acc,
    sem_head,
    xa_s, xa_r, zb_s, zb_r, xb_s, xb_r, yh_s, yh_r, zh_s, zh_r, xh_s, xh_r, xm_s, xm_r, ring_s, ring_r, zm_s, zm_r,
    sib_s, sib_r, sm_s, sm_r,
    hs_s, hs_r, st1_s, st1_r, st2_s, st2_r, td1_s, td1_r, td2_s, td2_r,
    y_s, y_r, f_s, f_r, l_s, l_r, sc_s, sc_r,
    p1_s, p1_r, p2_s, p2_r, rx_s, rx_r, rz_s, rz_r,
):
    v, y = lax.axis_index("vocab"), lax.axis_index("rows")
    z, x, c = lax.div(v, 8), lax.rem(lax.div(v, 2), 4), lax.rem(v, 2)
    oc = 1 - c

    def dev(dz=0, dx=0, dc=0, dy=0):
        zz = lax.rem(z + dz, NZ)
        xx = lax.rem(x + dx, NX)
        cc = c if dc == 0 else oc
        return (zz * 8 + xx * 2 + cc, lax.rem(y + dy, NY))

    started = []

    def send(src, dst, ss, rs, to):
        copy = pltpu.make_async_remote_copy(
            src_ref=src, dst_ref=dst, send_sem=ss, recv_sem=rs, device_id=to, device_id_type=MESH
        )
        copy.start()
        started.append(copy)
        return copy

    head_in = []
    for i in range(5):
        part_rows = pl.ds(i * 256, 256)
        copy = pltpu.make_async_copy(head_hbm.at[part_rows], head.at[part_rows], sem_head.at[i])
        copy.start()
        head_in.append(copy)

    xc = [(dx, dc) for dx in range(NX) for dc in range(NC) if (dx, dc) != (0, 0)]
    barrier = pltpu.get_barrier_semaphore()
    peers = [dev(dx=dx, dc=dc) for dx, dc in xc]
    peers += [dev(dz=d) for d in range(1, NZ)]
    peers += [dev(dy=d) for d in range(1, NY)]
    for to in peers:
        pl.semaphore_signal(barrier, inc=1, device_id=to, device_id_type=MESH)

    h = hidden[...].astype(F32)
    for own, at in ((own_a, 0), (own_b, DH)):
        own[...] = jnp.concatenate(
            [h[:, at + i * PW:at + (i + 1) * PW] for i in range(4)], axis=0
        ).astype(BF)
    for d in (1, 3, 2):
        yy = lax.rem(y + d, NY)
        hs = hidden[:, pl.ds(pl.multiple_of(yy * DS, DS), DS)].astype(F32)
        own_h[d - 1] = jnp.concatenate([hs[:, i * HW:(i + 1) * HW] for i in range(4)], axis=0).astype(BF)
    meta_own[0:4, :] = ids[...]
    meta_own[4:8, :] = probs[...]
    pl.semaphore_wait(barrier, len(peers))

    got_a = [send(own_a, buf_a.at[x], xa_s.at[d - 1], xa_r.at[d - 1], dev(dx=d)) for d in (1, 3, 2)]
    got_b = [send(own_b, buf_b.at[x, z], zb_s.at[d - 1], zb_r.at[d - 1], dev(dz=d)) for d in range(1, NZ)]
    base = c * 8 + z
    blk = base * 4 + x
    mine = meta.at[c, x, z]
    got_m = [send(meta_own, mine, zm_s.at[d - 1], zm_r.at[d - 1], dev(dz=d)) for d in range(1, NZ)]
    got_h = [
        send(own_h.at[d - 1], buf_h.at[x, z, d - 1], yh_s.at[d - 1], yh_r.at[d - 1], dev(dy=d)) for d in (1, 3, 2)
    ]
    buf_a[x] = own_a[...]
    buf_b[x, z] = own_b[...]
    meta[c, x, z] = meta_own[...]

    def rows_of(zz):
        return pl.ds(pl.multiple_of((c * 8 + zz) * 16, 16), 16)

    def lay_out(blocks, zz, at):
        blocks = [b.astype(F32) for b in blocks]
        for i in range(4):
            hid[rows_of(zz), at + i * PW:at + (i + 1) * PW] = jnp.concatenate(
                [b[4 * i:4 * i + 4] for b in blocks], axis=0
            ).astype(BF)

    sib = []

    def sib_send(zz, at):
        ref, n = hid.at[rows_of(zz), at:at + DH], len(sib)
        sib.append(send(ref, ref, sib_s.at[n], sib_r.at[n], dev(dc=1)))

    def ring_send(way, step):
        zz = lax.rem(z + (NZ - step if way == 0 else step), NZ)
        sent = []
        for n in range(RING):
            ref = hid.at[rows_of(zz), n * RW:(n + 1) * RW]
            sent.append(send(
                ref, ref, ring_s.at[way, step, n], ring_r.at[way, step, n], dev(dz=1 if way == 0 else NZ - 1)
            ))
        return sent

    got_xb = []

    def block_send(dz):
        zz = lax.rem(z + NZ - dz, NZ)
        if dz:
            got_b[dz - 1].wait_recv()
        ref = buf_b.at[x, zz]
        for d in (1, 3, 2):
            got_xb.append(send(ref, ref, xb_s.at[dz, d - 1], xb_r.at[dz, d - 1], dev(dx=d)))

    for copy in got_a:
        copy.wait_recv()
    lay_out([buf_a[i] for i in range(NX)], z, 0)
    now = [ring_send(0, 0), ring_send(1, 0)]
    sib_send(z, 0)
    slot = iota((64, SLOTS, TOPK), 1)
    lane3 = iota((64, SLOTS, TOPK), 2)
    got_l = {}

    def compact():
        got_sm.wait_recv()
        order = [(i, k, j) for i in range(NC) for j in range(NZ) for k in range(NX)]
        off = jnp.concatenate([meta[o][0:4] for o in order], axis=0) - v * VOC
        prob = jnp.concatenate([meta[o][4:8] for o in order], axis=0)
        mine = jnp.logical_and(off >= 0, off < VOC)
        mask = jnp.where(mine, 1.0, 0.0).astype(BF)
        before = jnp.where(iota((TOPK, TOPK), 0) < iota((TOPK, TOPK), 1), 1.0, 0.0).astype(BF)
        ri, rj = iota((GRP, GRP), 0), iota((GRP, GRP), 1)
        earlier = jnp.where(jnp.logical_and((ri >> 2) == (rj >> 2), rj < ri), 1.0, 0.0).astype(BF)
        count = jnp.dot(mask, jnp.ones((TOPK, TOPK), BF), preferred_element_type=F32).astype(BF)
        rank = jnp.dot(mask, before, preferred_element_type=F32)
        rank = rank + jnp.dot(earlier, count, preferred_element_type=F32)
        rank = jnp.where(mine, rank, -1.0).reshape(64, 4, TOPK)
        rows4 = iota((GRP, TOPK), 0) & 3
        code = (off * 4 + rows4).astype(F32).reshape(64, 4, TOPK)
        probf = prob.astype(F32).reshape(64, 4, TOPK)
        slot_f = slot.astype(F32)
        code_at = jnp.zeros((64, SLOTS, TOPK), F32)
        prob_at = jnp.zeros((64, SLOTS, TOPK), F32)
        for r in range(4):
            hit = rank[:, r:r + 1, :] == slot_f
            code_at = code_at + jnp.where(hit, code[:, r:r + 1, :], 0.0)
            prob_at = prob_at + jnp.where(hit, probf[:, r:r + 1, :], 0.0)
        code_c = jnp.sum(code_at, axis=2, keepdims=True)
        prob_c = jnp.sum(prob_at, axis=2, keepdims=True)
        lists[0] = jnp.sum(
            jnp.where(lane3 == slot, code_c, 0.0) + jnp.where(lane3 == slot + SLOTS, prob_c, 0.0), axis=1
        )
        for d in (1, 3, 2):
            got_l[d] = send(lists.at[0], lists.at[d], l_s.at[d - 1], l_r.at[d - 1], dev(dy=d))
        return code_c, prob_c

    for step in range(1, 5):
        for way in range(2):
            if way == 1 and step == 4:
                continue
            for copy in now[way]:
                copy.wait_recv()
            if step < (4 if way == 0 else 3):
                now[way] = ring_send(way, step)
            sib_send(lax.rem(z + (NZ - step if way == 0 else step), NZ), 0)
        if step == 1:
            for copy in got_m:
                copy.wait_recv()
            mine = meta.at[c, x]
            got_m = [send(mine, mine, xm_s.at[d - 1], xm_r.at[d - 1], dev(dx=d)) for d in (1, 3, 2)]
            for copy in got_b:
                copy.wait_recv()
            mine = buf_b.at[x]
            for d in (1, 3, 2):
                got_xb.append(send(mine, mine, xb_s.at[0, d - 1], xb_r.at[0, d - 1], dev(dx=d)))
        if step == 2:
            for copy in got_m:
                copy.wait_recv()
            mine = meta.at[c]
            got_sm = send(mine, mine, sm_s, sm_r, dev(dc=1))
        if step == 2:
            for copy in got_h:
                copy.wait_recv()
            mine = buf_h.at[x, z]
            got_h = [send(mine, mine, zh_s.at[d - 1], zh_r.at[d - 1], dev(dz=d)) for d in range(1, NZ)]
        if step == 3:
            code_c, prob_c = compact()
    for copy in got_h:
        copy.wait_recv()
    mine = buf_h.at[x]
    got_h = [send(mine, mine, xh_s.at[d - 1], xh_r.at[d - 1], dev(dx=d)) for d in (1, 3, 2)]
    for copy in got_xb:
        copy.wait_recv()
    for zz in range(NZ):
        lay_out([buf_b[i, zz] for i in range(NX)], zz, DH)
        sib_send(zz, DH)

    half = pl.ds(pl.multiple_of(c * 128, 128), 128)

    for copy in head_in:
        copy.wait()
    for copy in sib[:8]:
        copy.wait_recv()
    for n in range(5):
        ns = slice(n * 256, (n + 1) * 256)
        logits[:, ns] = lax.dot_general(
            hid[:, 0:DH], head[ns, 0:DH], (((1,), (1,)), ((), ())), preferred_element_type=F32
        )
    for copy in sib[8:]:
        copy.wait_recv()
    for n in range(5):
        ns = slice(n * 256, (n + 1) * 256)
        logits[:, ns] += lax.dot_general(
            hid[:, DH:D], head[ns, DH:D], (((1,), (1,)), ((), ())), preferred_element_type=F32
        )
    lg = logits[...]
    m_own = jnp.max(lg, axis=1, keepdims=True)
    ex = jnp.exp(lg - m_own)
    e_buf[0] = ex.astype(BF)
    s_own = jnp.sum(ex, axis=1, keepdims=True)
    my_row = blk * 4
    row_id = iota((GRP, 128), 0)
    lane = iota((GRP, 128), 1)
    w_own = jnp.zeros((GRP, 128), F32)
    for r in range(4):
        w_own = jnp.where(row_id == my_row + r, weight[r], w_own)
    wide = jnp.where(lane == 0, m_own, jnp.where(lane == 1, s_own, w_own))
    packet[...] = wide.T[0:8, :]

    def combine(buf):
        top = buf[0, 0:1, :]
        for i in range(1, 8):
            top = jnp.maximum(top, buf[i, 0:1, :])
        total = [jnp.zeros((1, GRP), F32) for _ in range(2)]
        for i in range(8):
            total[0] = total[0] + buf[i, 1:2, :] * jnp.exp(buf[i, 0:1, :] - top)
            total[1] = total[1] + buf[i, 2:3, :]
        sub = iota((8, GRP), 0)
        return jnp.where(sub == 0, top, jnp.where(sub == 1, total[0], total[1]))

    place = x * 2 + c

    def over_xc(own, buf, ss, rs):
        got = [
            send(own, buf.at[place], ss.at[i], rs.at[i], dev(dx=dx, dc=dc))
            for i, (dx, dc) in enumerate(xc)
        ]
        buf[place] = own[...]
        return got

    def over_z(buf, ss, rs):
        mid = buf.at[z]
        return [send(mid, mid, ss.at[d - 1], rs.at[d - 1], dev(dz=d)) for d in range(1, NZ)]

    got = over_xc(packet, st1, st1_s, st1_r)

    got_y = {}

    def y_send(k):
        ks = pl.ds(*YCH[k])
        for d in (1, 3):
            got_y[d, k] = [send(
                e_buf.at[0, :, ks], e_buf.at[d, :, ks], y_s.at[d - 1, k], y_r.at[d - 1, k], dev(dy=d)
            )]

    y_send(0)

    def forward(k):
        ks = pl.ds(*YCH[k])
        got_y[2, k] = []
        for d, n in ((1, 0), (3, 1)):
            got_y[d, k].pop().wait_recv()
            rows = pl.ds(n * 128, 128)
            got_y[2, k].append(send(
                e_buf.at[d, rows, ks], e_buf.at[2, rows, ks], f_s.at[n, k], f_r.at[n, k], dev(dy=d)
            ))

    i0 = iota((GRP, GRP), 0)
    src = ((i0 >> 7) << 7) + (((i0 >> 2) & 7) << 4) + (((i0 >> 5) & 3) << 2) + (i0 & 3)
    perm = jnp.where(src == iota((GRP, GRP), 1), 1.0, 0.0).astype(BF)
    other = pl.ds(pl.multiple_of(oc * 128, 128), 128)
    got_p1, got_x, got_z = {}, {}, {}

    def pair_send(q, part, p_send, p_recv, ss, rs, left):
        at, width = CHUNKS[q]
        qs = slice(at, at + width)
        part[:, qs] = jnp.dot(left[...], head[:, qs], preferred_element_type=F32)
        p_send[:, qs] = part[other, qs].astype(BF)
        return send(p_send.at[:, qs], p_recv.at[:, qs], ss, rs, dev(dc=1))

    ep[...] = jnp.dot(perm, e_buf[0], preferred_element_type=F32).astype(BF)
    got_p1[0] = pair_send(0, part1, p1_send, p1_recv, p1_s.at[0], p1_r.at[0], ep)
    for copy in got:
        copy.wait_recv()
    st2[z] = combine(st1)
    got = over_z(st2, st2_s, st2_r)

    lanes = iota((256, 128), 1)
    places = iota((256, VOC), 1)
    block_row = (iota((256, 128), 0) >> 4) << 2

    def make_teacher(code_c, prob_c, width):
        code_i = code_c.reshape(64 * SLOTS, 1).astype(I32)
        prob_i = prob_c.reshape(64 * SLOTS, 1).astype(I32)
        for b in range(4):
            code_b, prob_b = code_i[b * 256:(b + 1) * 256], prob_i[b * 256:(b + 1) * 256]
            one_hot = jnp.where((code_b >> 2) == places[:, 0:width], 1.0, 0.0).astype(BF)
            byte = jnp.where(lanes < 64, prob_b >> 8, prob_b & 255).astype(F32)
            at = jnp.where((lanes & 63) == block_row + (code_b & 3), byte, 0.0).astype(BF)
            both = lax.dot_general(at, one_hot, (((0,), (0,)), ((), ())), preferred_element_type=F32)
            teacher[b * 64:(b + 1) * 64, 0:width] = (both[0:64] * 256.0 + both[64:128]) * (1.0 / 65536.0)

    def other_teacher(d):
        got_l[d].wait_recv()
        flat = jnp.broadcast_to(lists[d][:, None, :], (64, SLOTS, TOPK))
        make_teacher(
            jnp.sum(jnp.where(lane3 == slot, flat, 0.0), axis=2, keepdims=True),
            jnp.sum(jnp.where(lane3 == slot + SLOTS, flat, 0.0), axis=2, keepdims=True),
            YCH[0][1],
        )

    make_teacher(code_c, prob_c, VOC)
    tp[...] = jnp.dot(perm, teacher[...].astype(BF), preferred_element_type=F32).astype(BF)
    got_p2 = pair_send(0, part2, p2_send, p2_recv, p2_s, p2_r, tp)
    t_own = jnp.sum(teacher[...] * logits[...], axis=1, keepdims=True)
    packet2[...] = jnp.broadcast_to(t_own, (GRP, 128)).T[0:8, :]
    got_td = over_xc(packet2, td1, td1_s, td1_r)
    for copy in got:
        copy.wait_recv()

    final = combine(st2)
    top, ratio, w_row = final[0:1, :], final[2:3, :] / final[1:2, :], final[2:3, :]
    a_row = jnp.exp(packet[0:1, :] - top) * ratio
    b_row = jnp.exp(st1[x * 2 + oc, 0:1, :] - top) * ratio
    scales[0] = jnp.concatenate([a_row, w_row, b_row, final[0:2, :], jnp.zeros((3, GRP), F32)], axis=0)
    got_sc = {
        d: send(scales.at[0], scales.at[d], sc_s.at[d - 1], sc_r.at[d - 1], dev(dy=d)) for d in (1, 3, 2)
    }

    def columns(d):
        return jnp.concatenate([scales[d], jnp.zeros((120, GRP), F32)], axis=0).T

    cols[...] = columns(0)
    scale_c[...] = jnp.concatenate(
        [
            cols[i * 128 + k * 16 + j * 4:i * 128 + k * 16 + j * 4 + 4, :]
            for i in range(NC) for j in range(NX) for k in range(NZ)
        ],
        axis=0,
    )

    def x_stage(q):
        at, width = CHUNKS[q]
        qs = slice(at, at + width)
        got_p1[q].wait_recv()
        if q == 0:
            got_p2.wait_recv()
            sc = scale_c[half, :]
            total = sc[:, 0:1] * part1[half, qs] + sc[:, 2:3] * p1_recv[:, qs].astype(F32)
            total = total - sc[:, 1:2] * (part2[half, qs] + p2_recv[...].astype(F32))
        else:
            total = part1[half, qs] + p1_recv[:, qs].astype(F32)
        s1[:, qs] = total
        x_send[:, qs] = total.astype(BF)
        for d in (1, 3, 2):
            xx = lax.rem(x + d, NX)
            rows = pl.ds(pl.multiple_of(xx * 32, 32), 32)
            got_x[q, d] = send(
                x_send.at[rows, qs], x_recv.at[d - 1, :, qs], rx_s.at[q, d - 1], rx_r.at[q, d - 1], dev(dx=d)
            )

    def pair_stage(q):
        got_p1[q] = pair_send(q, part1, p1_send, p1_recv, p1_s.at[q], p1_r.at[q], ep)

    def z_stage(q):
        at, width = CHUNKS[q]
        qs = slice(at, at + width)
        w4 = width // 4
        zs = slice(at // 4, at // 4 + w4)
        for d in (1, 3, 2):
            got_x[q, d].wait_recv()
        s2 = s1[pl.ds(pl.multiple_of(x * 32, 32), 32), qs]
        for d in range(3):
            s2 = s2 + x_recv[d, :, qs].astype(F32)
        for zz in range(NZ):
            piece = jnp.concatenate([s2[4 * zz:4 * zz + 4, i * w4:(i + 1) * w4] for i in range(4)], axis=0)
            z_f32[zz, :, zs] = piece
            z_send[zz, :, zs] = piece.astype(BF)
        for d in range(1, NZ):
            zz = lax.rem(z + d, NZ)
            got_z[q, d] = send(
                z_send.at[zz, :, zs], z_recv.at[d - 1, :, zs], rz_s.at[q, d - 1], rz_r.at[q, d - 1], dev(dz=d)
            )

    def last_stage(q):
        at, width = CHUNKS[q]
        w4 = width // 4
        zs = slice(at // 4, at // 4 + w4)
        for d in range(1, NZ):
            got_z[q, d].wait_recv()
        total = z_f32[z, :, zs]
        for d in range(NZ - 1):
            total = total + z_recv[d, :, zs].astype(F32)
        row_out[:, at:at + width] = jnp.concatenate(
            [total[4 * i:4 * i + 4] for i in range(4)], axis=1
        ).astype(BF)

    def head_step(d, k):
        at, width = YCH[k]
        ks = slice(at, at + width)
        if d == 0:
            left, sc = hid[:, pl.ds(pl.multiple_of(y * DS, DS), DS)], cols
        else:
            left, sc = hy[d - 1], scale_c
            for copy in got_y[d, k]:
                copy.wait_recv()
        if k == 0:
            grad[...] = (
                sc[:, 0:1] * e_buf[d, :, ks].astype(F32) - sc[:, 1:2] * teacher[:, ks]
            ).astype(BF)
            right = grad[...]
        else:
            right = e_buf[d, :, ks]
        term = lax.dot_general(left, right, (((0,), (0,)), ((), ())), preferred_element_type=F32)
        if d == 0:
            acc[:, ks] = term
        elif d != 2:
            acc[:, ks] += term
        else:
            head_out[:, ks] = (acc[:, ks] + term).astype(BF)

    def prepare(d):
        other_teacher(d)
        got_sc[d].wait_recv()
        scale_c[...] = columns(d)

    x_stage(0)
    late = slice(YCH[1][0], YCH[1][0] + YCH[1][1])
    e_buf[0, :, late] = (
        cols[:, 0:1] * e_buf[0, :, late].astype(F32) - cols[:, 1:2] * teacher[:, late]
    ).astype(BF)
    y_send(1)
    ep[...] = (scale_c[:, 0:1] * ep[...].astype(F32) - scale_c[:, 1:2] * tp[...].astype(F32)).astype(BF)
    pair_stage(1)
    pair_stage(2)
    x_stage(1)
    pair_stage(3)
    x_stage(2)
    x_stage(3)
    forward(0)
    head_step(0, 0)
    head_step(0, 1)
    for copy in got_td:
        copy.wait_recv()
    td2[z] = jnp.sum(td1[...], axis=0)
    got_td = over_z(td2, td2_s, td2_r)
    for copy in got_h:
        copy.wait_recv()
    got_hs = []
    for d in (1, 3, 2):
        for zz in range(NZ):
            blocks = [buf_h[j, zz, d - 1].astype(F32) for j in range(NX)]
            for i in range(4):
                hy[d - 1, rows_of(zz), i * HW:(i + 1) * HW] = jnp.concatenate(
                    [b[4 * i:4 * i + 4] for b in blocks], axis=0
                ).astype(BF)
        ref = hy.at[d - 1, half]
        got_hs.append(send(ref, ref, hs_s.at[d - 1], hs_r.at[d - 1], dev(dc=1)))
    z_stage(0)
    prepare(1)
    for copy in got_hs:
        copy.wait_recv()
    head_step(1, 0)
    z_stage(1)
    prepare(3)
    head_step(3, 0)
    z_stage(2)
    forward(1)
    head_step(1, 1)
    head_step(3, 1)
    z_stage(3)
    prepare(2)
    for k in range(YC):
        head_step(2, k)
    for q in range(NQ):
        last_stage(q)
    for copy in got_td:
        copy.wait_recv()
    dots = jnp.concatenate([jnp.sum(td2[...], axis=0), jnp.zeros((120, GRP), F32)], axis=0).T
    dot_buf[...] = dots
    mine = pl.ds(pl.multiple_of(my_row, 4), 4)
    own_cols = cols[mine, :]
    own_loss = own_cols[:, 3:4] + jnp.log(own_cols[:, 4:5]) - dot_buf[mine, :][:, 0:1]
    at_lane = iota((4, 128), 0) == iota((4, 128), 1)
    loss_out[...] = jnp.sum(jnp.where(at_lane, own_loss, 0.0), axis=0)[0:4]
    for copy in started:
        copy.wait_send()


def shards(hidden, head, row_weight, teacher_ids, teacher_probs):
    dma = pltpu.SemaphoreType.DMA
    vm = pltpu.VMEM
    any_spec = pl.BlockSpec(memory_space=pl.ANY)
    vm_spec = pl.BlockSpec(memory_space=pltpu.VMEM)
    return pl.pallas_call(
        kernel,
        out_shape=(
            vm((4, D), BF),
            vm((4,), F32),
            vm((DS, VOC), BF),
        ),
        in_specs=[vm_spec, any_spec, pl.BlockSpec(memory_space=pltpu.SMEM), vm_spec, vm_spec],
        out_specs=(vm_spec, vm_spec, vm_spec),
        scratch_shapes=[
            vm((VOC, D), BF), vm((16, PW), BF), vm((16, PW), BF), vm((3, 16, HW), BF),
            vm((NX, 16, PW), BF), vm((NX, NZ, 16, PW), BF), vm((NX, NZ, 3, 16, HW), BF), vm((GRP, D), BF),
            vm((8, 128), I32), vm((NC, NX, NZ, 8, 128), I32), vm((3, GRP, DS), BF),
            vm((GRP, VOC), F32), vm((GRP, VOC), F32), vm((4, 64, TOPK), F32),
            vm((8, GRP), F32), vm((8, 8, GRP), F32), vm((8, 8, GRP), F32), vm((GRP, 128), F32),
            vm((8, GRP), F32), vm((8, 8, GRP), F32), vm((8, 8, GRP), F32), vm((GRP, 128), F32),
            vm((4, 8, GRP), F32), vm((GRP, 128), F32),
            vm((4, GRP, VOC), BF), vm((GRP, YCH[0][1]), BF), vm((GRP, VOC), BF), vm((GRP, VOC), BF),
            vm((GRP, D), F32), vm((GRP, CHUNKS[0][1]), F32),
            vm((128, D), BF), vm((128, D), BF), vm((128, CHUNKS[0][1]), BF), vm((128, CHUNKS[0][1]), BF),
            vm((128, D), F32), vm((128, D), BF), vm((3, 32, D), BF),
            vm((NZ, 16, D // 4), F32), vm((NZ, 16, D // 4), BF), vm((NZ - 1, 16, D // 4), BF),
            vm((DS, VOC), F32),
            dma((5,)),
            dma((3,)), dma((3,)), dma((7,)), dma((7,)), dma((1, 3)), dma((1, 3)),
            dma((3,)), dma((3,)), dma((7,)), dma((7,)), dma((3,)), dma((3,)), dma((3,)), dma((3,)),
            dma((2, 4, RING)), dma((2, 4, RING)), dma((7,)), dma((7,)), dma((16,)), dma((16,)), dma, dma,
            dma((3,)), dma((3,)), dma((7,)), dma((7,)), dma((7,)), dma((7,)),
            dma((7,)), dma((7,)), dma((7,)), dma((7,)),
            dma((3, YC)), dma((3, YC)), dma((2, YC)), dma((2, YC)),
            dma((3,)), dma((3,)), dma((3,)), dma((3,)),
            dma((NQ,)), dma((NQ,)), dma, dma, dma((NQ, 3)), dma((NQ, 3)), dma((NQ, 7)), dma((NQ, 7)),
        ],
        compiler_params=pltpu.CompilerParams(
            collective_id=0, has_side_effects=True, vmem_limit_bytes=52 << 20
        ),
        cost_estimate=pl.CostEstimate(flops=8_100_000_000, bytes_accessed=14_000_000, transcendentals=330_000),
    )(hidden, head, row_weight, teacher_ids, teacher_probs)


def solution(mesh):
    in_specs = (
        P(("vocab", "rows"), None),
        P("vocab", None),
        P(("vocab", "rows")),
        P(("vocab", "rows"), None),
        P(("vocab", "rows"), None),
    )
    out_specs = (P(("vocab", "rows"), None), P(("vocab", "rows")), P("rows", "vocab"))
    return jax.shard_map(shards, mesh=mesh, in_specs=in_specs, out_specs=out_specs, check_vma=False)
```
